256 devices in a mesh: row: 16 (over x, y), col: 16 (over z, core).
Axes of the slice: x: 4, y: 4, z: 8, core: 2. Of those that a mesh axis runs over, the one named last changes fastest.
Arguments:
- patches: bfloat16 [4096, 3072], P('row', 'col'), may hold values from -47 to 47
- norm_gain: float32 [3072], P('col'), may hold values from 0.1 to 1.9
- up_weight: bfloat16 [3072, 12288], P('row', 'col'), may hold values from -0.109375 to 0.109375
- up_bias: float32 [12288], P('col'), may hold values from -3 to 3
- down_weight: bfloat16 [12288, 3072], P('col', 'row'), may hold values from -0.0546875 to 0.0546875
- down_bias: float32 [3072], P('col'), may hold values from -3 to 3
- cotangent: bfloat16 [4096, 3072], P('row', 'col'), may hold values from -6 to 6
Outputs:
- mixed: bfloat16 [4096, 3072], P('row', 'col')
- patch_grad: bfloat16 [4096, 3072], P('row', 'col')
- gain_grad: float32 [3072], P('col')
- up_weight_grad: bfloat16 [3072, 12288], P('row', 'col')
- up_bias_grad: float32 [12288], P('col')
- down_weight_grad: bfloat16 [12288, 3072], P('col', 'row')
- down_bias_grad: float32 [3072], P('row')
The draws below stay inside these ranges and needn't reach their ends.
All inputs are finite; a program needn't handle non-finite values.
Results may differ from the reference program's by a relative error of at most 0.023.
Values may be sent and summed in bfloat16 or wider, within the bound.
A program may use at most 64 MiB of HBM per device.

```python
import math
import jax
import jax.numpy as jnp
from jax import lax

D = 3072
F = 12288
TOK_DEV = 256
TOKENS = 4096
N_ROW = 16


def draw_patches(key, part):
    key = jax.random.fold_in(key, 11)
    key_rows, key_cols, key_base = jax.random.split(key, 3)
    row_scale = 10.0 ** jax.random.uniform(key_rows, (TOKENS, 1), minval=-0.5, maxval=0.5)
    ramp = jnp.arange(D, dtype=jnp.float32) / (D - 1)
    col_scale = (10.0 ** (ramp - 0.5))[None, :] * jax.random.uniform(key_cols, (1, D), minval=0.7, maxval=1.4)
    base = jax.random.truncated_normal(key_base, -3.0, 3.0, (TOKENS, D))
    return (base * row_scale * col_scale).astype(jnp.bfloat16)


def with_spikes(entries, own_key, source, target, shards_of, factor):
    def block_of(dim):
        return (jnp.arange(entries.shape[dim]) // (entries.shape[dim] // shards_of)).reshape((-1,) + (1,) * (entries.ndim - 1 - dim))

    near = jax.random.permutation(own_key, shards_of)[block_of(target)]
    other_side = (block_of(target) + shards_of // 2) % shards_of
    return jnp.where((block_of(source) == near) | (block_of(source) == other_side), factor * entries, entries)


def block_levels(key, shape, shards, low, high):
    loudness = 1.0
    for dim, blocks in shards:
        heights = jax.random.uniform(jax.random.fold_in(jax.random.fold_in(key, 6), dim), (blocks,), jnp.float32, low / len(shards), high / len(shards))
        loudness = loudness * jnp.repeat(jnp.exp(heights), shape[dim] // blocks).reshape((-1,) + (1,) * (len(shape) - 1 - dim))
    return loudness


def normal_values(key, extent, scale, limit, cuts=(), kind=jnp.bfloat16):
    values = scale * jax.random.normal(key, extent, jnp.float32)
    if cuts:
        values = values * block_levels(key, extent, cuts, -0.22, 0.18)
    return jnp.clip(values, -limit, limit).astype(kind)


def heavy_noise(rng, dims, width, limit, cuts, heavy, kind=jnp.bfloat16):
    values = width * jax.random.normal(rng, dims, jnp.float32)
    if cuts:
        values = values * block_levels(rng, dims, cuts, -0.22, 0.18)
    return jnp.clip(with_spikes(values, jax.random.fold_in(rng, 3), *heavy), -limit, limit).astype(kind)


def setup_inputs(seed: int = 0) -> dict:
    key_of = jax.random.split(jax.random.key(seed), 8)
    patches = draw_patches(jax.random.fold_in(key_of[7], 71), 0)
    norm_gain = jnp.clip(1.0 + 0.18 * jax.random.normal(key_of[1], (D,), jnp.float32), 0.1, 1.9)
    up_weight = normal_values(key_of[2], (D, F), D ** -0.5, 0.109375, ((0, 16), (1, 16)))
    up_bias = normal_values(key_of[3], (F,), 0.5, 3.0, ((0, 16),), jnp.float32)
    down_weight = normal_values(key_of[4], (F, D), F ** -0.5, 0.0546875, ((0, 16), (1, 16)))
    down_bias = normal_values(key_of[5], (D,), 0.5, 3.0, ((0, 16),), jnp.float32)
    cotangent = heavy_noise(key_of[6], (TOKENS, D), 1.0, 6.0, ((0, 16), (1, 16)), (0, 1, 16, 2.0))
    return {"patches": patches, "norm_gain": norm_gain, "up_weight": up_weight, "up_bias": up_bias, "down_weight": down_weight, "down_bias": down_bias, "cotangent": cotangent}


def gelu_slope(pre_act):
    cdf_part = 0.5 * (1.0 + lax.erf(pre_act * 0.7071067811865476))
    return cdf_part + pre_act * jnp.exp(-0.5 * pre_act * pre_act) * 0.3989422804014327

def reference(patches, norm_gain, up_weight, up_bias, down_weight, down_bias, cotangent):
    inputs = patches.astype(jnp.float32)
    row_mean = lax.optimization_barrier(jnp.mean(inputs, axis=1, keepdims=True))
    centred = inputs - row_mean
    row_var = lax.optimization_barrier(jnp.mean(centred * centred, axis=1, keepdims=True))
    inv_std = lax.rsqrt(row_var + 1e-06)
    normed = centred * inv_std
    normed_bf = (normed * norm_gain[None, :]).astype(jnp.bfloat16)
    pre_act = jnp.dot(normed_bf, up_weight, preferred_element_type=jnp.float32) + up_bias[None, :]
    hidden = jax.nn.gelu(pre_act, approximate=False).astype(jnp.bfloat16)
    mixed = (inputs + jnp.dot(hidden, down_weight, preferred_element_type=jnp.float32) + down_bias[None, :]).astype(jnp.bfloat16)
    hidden_grad = jnp.dot(cotangent, down_weight.T, preferred_element_type=jnp.float32)
    pre_grad = (hidden_grad * gelu_slope(pre_act)).astype(jnp.bfloat16)
    grad_scale = 1.0 / math.sqrt(TOKENS)

    def block_terms(index, carry):
        up_total, down_total, bias_total = carry
        start = (index * TOK_DEV).astype(jnp.int32)
        normed_rows = lax.dynamic_slice_in_dim(normed_bf, start, TOK_DEV, 0)
        grad_rows = lax.dynamic_slice_in_dim(pre_grad, start, TOK_DEV, 0)
        hidden_rows = lax.dynamic_slice_in_dim(hidden, start, TOK_DEV, 0)
        cot_rows = lax.dynamic_slice_in_dim(cotangent, start, TOK_DEV, 0)
        up_term = (grad_scale * jnp.dot(normed_rows.T, grad_rows, preferred_element_type=jnp.float32)).astype(jnp.bfloat16)
        down_term = (grad_scale * jnp.dot(hidden_rows.T, cot_rows, preferred_element_type=jnp.float32)).astype(jnp.bfloat16)
        bias_term = (grad_scale * lax.optimization_barrier(jnp.sum(cot_rows.astype(jnp.float32), axis=0))).astype(jnp.bfloat16)
        up_term, down_term, bias_term = lax.optimization_barrier((up_term, down_term, bias_term))
        return (up_total + up_term.astype(jnp.float32), down_total + down_term.astype(jnp.float32), bias_total + bias_term.astype(jnp.float32))
    start_carry = (jnp.zeros((D, F), jnp.float32), jnp.zeros((F, D), jnp.float32), jnp.zeros((D,), jnp.float32))
    up_total, down_total, bias_total = lax.fori_loop(0, N_ROW, block_terms, start_carry)
    normed_grad = jnp.dot(pre_grad, up_weight.T, preferred_element_type=jnp.float32)
    up_bias_grad = grad_scale * lax.optimization_barrier(jnp.sum(pre_grad.astype(jnp.float32), axis=0))
    gain_grad = grad_scale * lax.optimization_barrier(jnp.sum(normed_grad * normed, axis=0))
    scaled_grad = normed_grad * norm_gain[None, :]
    first_mean = lax.optimization_barrier(jnp.mean(scaled_grad, axis=1, keepdims=True))
    second_mean = lax.optimization_barrier(jnp.mean(scaled_grad * normed, axis=1, keepdims=True))
    patch_grad = (cotangent.astype(jnp.float32) + inv_std * (scaled_grad - first_mean - normed * second_mean)).astype(jnp.bfloat16)
    return (mixed, patch_grad, gain_grad, up_total.astype(jnp.bfloat16), up_bias_grad, down_total.astype(jnp.bfloat16), bias_total)
```

```python
import functools
import math

import jax
import jax.numpy as jnp
from jax import lax
from jax.experimental import pallas as pl
from jax.experimental.pallas import tpu as pltpu
from jax.sharding import PartitionSpec as P

MESH = pl.DeviceIdType.MESH
BF = jnp.bfloat16
F32 = jnp.float32

NB = 16
FB = 192
TB = 256
HB = 384
D = NB * FB
N_SEM = 320


def rem(a, n):
    return lax.rem(a, n)


def tn_dot(left, right):
    return lax.dot_general(
        left, right, (((0,), (0,)), ((), ())), preferred_element_type=F32
    )


def nn_dot(left, right):
    return jnp.dot(left, right, preferred_element_type=F32)


def kernel(
    scale,
    patches, gain, w1in, ubias, w2in, dbias, cot,
    mixed_o, pgrad_o, gaing_o, dw1_o, ubg_o, dw2_o, dbg_o,
    XT, XN, CT, W1, W2, W1H, W2H,
    GA, UB, BC, GW, MI,
    PRE, SL, HG, HID, PG, HIDR, PGR,
    MX, MXS, MXP, MXM, MXT,
    NG, NGS, NGP, NGM, NGT,
    G1, G1Y, G1X, G1T, G1F,
    G2, G2Y, G2X, G2T, G2F,
    ST, STS, STZ, STT,
    MS, RM, UT, FU, GT, GTX, GTY,
    ss, rs,
):
    r = lax.axis_index("row")
    c = lax.axis_index("col")
    x, y = r // 4, rem(r, 4)
    z, k = c // 2, rem(c, 2)
    g = y // 2
    yh = y + 1 - 2 * rem(y, 2)
    yt = 3 - y
    own = g == k
    other = g != k

    def dev(xx, yy, zz, kk):
        return (xx * 4 + yy, zz * 2 + kk)

    def zdev(j):
        return dev(x, y, rem(z + j + 8, 8), k)

    def xdev(j):
        return dev(rem(x + j + 4, 4), y, z, k)

    sib = dev(x, y, z, 1 - k)
    hdev = dev(x, yh, z, k)
    tdev = dev(x, yt, z, k)
    tdev2 = dev(x, yt, z, 1 - k)

    def zb(j, kk):
        return rem(z + j + 8, 8) * 2 + kk

    def wb(j, yy):
        return rem(x + j + 4, 4) * 4 + yy

    b0 = zb(0, k)

    ids = {}
    made = {}

    def sem(name):
        return ids.setdefault(name, len(ids))

    def rc(sname, rname, src, dst, to):
        return pltpu.make_async_remote_copy(
            src_ref=src, dst_ref=dst, send_sem=ss.at[sem(sname)], recv_sem=rs.at[sem(rname)],
            device_id=to, device_id_type=MESH,
        )

    def send(name, src, dst, to):
        copy = rc(name, name, src, dst, to)
        copy.start()
        made[name] = copy

    def got(*names):
        for name in names:
            made[name].wait_recv()

    barrier = pltpu.get_barrier_semaphore()
    peers = [zdev(j) for j in range(1, 8)] + [xdev(j) for j in range(1, 4)]
    peers += [dev(x, rem(y + j, 4), z, k) for j in range(1, 4)]
    peers += [dev(rem(x + j, 4), yh, z, k) for j in range(1, 4)]
    peers += [sib, tdev2]
    for peer in peers:
        pl.semaphore_signal(barrier, inc=1, device_id=peer, device_id_type=MESH)

    XT[0, b0] = patches[...].T
    W1H[0] = w1in[:, :HB]
    W1H[1] = w1in[:, HB:]
    GA[k, z] = jnp.zeros((8, 256), F32)
    GA[k, z, :, 0:FB] = jnp.broadcast_to(gain[...], (8, FB))
    UB[0] = jnp.broadcast_to(ubias[:, pl.ds(pl.multiple_of(k * HB, 128), HB)], (8, HB))
    UB[1] = jnp.broadcast_to(ubias[:, pl.ds(pl.multiple_of((1 - k) * HB, 128), HB)], (8, HB))
    pl.semaphore_wait(barrier, len(peers))

    def tok_edge(t, A):
        send(t + "T", A.at[0, b0], A.at[1, b0], tdev)

    def tok_first(t, A, s):
        send(f"{t}p1{s}", A.at[s, b0], A.at[s, b0], zdev(1))
        send(f"{t}m1{s}", A.at[s, b0], A.at[s, b0], zdev(-1))
        send(f"{t}sib0{s}", A.at[s, b0], A.at[s, b0], sib)

    def tok_next(t, A, s, n):
        bp, bm = zb(-n, k), zb(n, k)
        got(f"{t}p{n}{s}")
        if n < 3:
            send(f"{t}p{n + 1}{s}", A.at[s, bp], A.at[s, bp], zdev(1))
        else:
            half = pl.ds(0, FB // 2)
            send(f"{t}p4{s}", A.at[s, bp, half], A.at[s, bp, half], zdev(1))
        got(f"{t}m{n}{s}")
        if n < 3:
            send(f"{t}m{n + 1}{s}", A.at[s, bm], A.at[s, bm], zdev(-1))
        else:
            half = pl.ds(FB // 2, FB // 2)
            send(f"{t}m4{s}", A.at[s, bm, half], A.at[s, bm, half], zdev(-1))
        send(f"{t}sibp{n}{s}", A.at[s, bp], A.at[s, bp], sib)
        send(f"{t}sibm{n}{s}", A.at[s, bm], A.at[s, bm], sib)

    def tok_last(t, A, s):
        b4 = zb(4, k)
        got(f"{t}p4{s}", f"{t}m4{s}")
        send(f"{t}sib4{s}", A.at[s, b4], A.at[s, b4], sib)

    def tok_done(t, s):
        for n in ("0", "p1", "m1", "p2", "m2", "p3", "m3", "4"):
            got(f"{t}sib{n}{s}")

    r0, rt = wb(0, y), wb(0, yt)

    def w_start(t, WH, W):
        @pl.when(own)
        def _():
            W[r] = WH[k]
            rc(t + "b", t + "u0", WH.at[1 - k], W.at[r], sib).start()

        @pl.when(other)
        def _():
            rc(t + "a", t + "u1", WH.at[k], W.at[r], tdev).start()
            rc(t + "b", t + "u1", WH.at[1 - k], W.at[r], tdev2).start()

    def w_u0(t, WH, W):
        @pl.when(other)
        def _():
            rc(t + "b", t + "u0", WH.at[1 - k], W.at[r], sib).wait_recv()

        send(t + "P+", W.at[r0], W.at[r0], xdev(1))
        send(t + "P-", W.at[r0], W.at[r0], xdev(-1))
        send(t + "Y0", W.at[r0], W.at[r0], hdev)

    def w_u1(t, WH, W):
        rc(t + "a", t + "u1", WH.at[k], W.at[rt], tdev).wait_recv()
        send(t + "Q0", W.at[rt], W.at[rt], hdev)
        send(t + "Q+", W.at[rt], W.at[rt], xdev(1))
        send(t + "Q-", W.at[rt], W.at[rt], xdev(-1))

    lo, hi = pl.ds(0, FB // 2), pl.ds(FB // 2, FB // 2)

    def w_half(t, n, W, yy, relay):
        bp, bm = wb(-1, yy), wb(1, yy)
        got(f"{t}{n}+")
        send(f"{t}{n}2+", W.at[bp, lo], W.at[bp, lo], xdev(1))
        got(f"{t}{n}-")
        send(f"{t}{n}2-", W.at[bm, hi], W.at[bm, hi], xdev(-1))
        if relay:
            send(t + "Y1", W.at[bp], W.at[bp], hdev)
            send(t + "Y2", W.at[bm], W.at[bm], hdev)

    def w_p1(t, W):
        w_half(t, "P", W, y, True)

    def w_q0(t, W):
        b = wb(0, 3 - yh)
        got(t + "Q0")
        send(t + "R+", W.at[b], W.at[b], xdev(1))
        send(t + "R-", W.at[b], W.at[b], xdev(-1))

    def w_q1(t, W):
        w_half(t, "Q", W, yt, False)

    def w_r1(t, W):
        w_half(t, "R", W, 3 - yh, False)

    def w_p2(t, W):
        b = wb(2, y)
        got(t + "P2+", t + "P2-")
        send(t + "Y3", W.at[b], W.at[b], hdev)

    def w_done(t):
        got(*(t + n for n in ("Q2+", "Q2-", "R2+", "R2-", "Y0", "Y1", "Y2", "Y3")))

    tok_edge("X", XT)
    tok_first("X", XT, 0)
    w_start("V", W1H, W1)
    CT[0, b0] = cot[...].T
    W2H[0] = w2in[:HB].T
    W2H[1] = w2in[HB:].T
    send("ub", UB.at[1], UB.at[2], sib)
    for j in range(1, 8):
        send(f"ga{j}", GA.at[k, z], GA.at[k, z], zdev(j))
    w_u0("V", W1H, W1)
    got("XT")
    tok_first("X", XT, 1)
    tok_edge("C", CT)
    w_start("U", W2H, W2)
    tok_next("X", XT, 0, 1)
    w_u1("V", W1H, W1)
    w_p1("V", W1)
    tok_next("X", XT, 1, 1)
    tok_first("C", CT, 0)
    tok_next("X", XT, 0, 2)
    w_q0("V", W1)
    w_q1("V", W1)
    w_u0("U", W2H, W2)
    tok_next("X", XT, 1, 2)
    tok_next("X", XT, 0, 3)
    got("CT")
    tok_first("C", CT, 1)
    w_u1("U", W2H, W2)
    w_p2("V", W1)
    tok_next("X", XT, 1, 3)
    w_r1("V", W1)
    tok_next("C", CT, 0, 1)
    tok_last("X", XT, 0)
    w_p1("U", W2)
    tok_next("C", CT, 1, 1)
    tok_last("X", XT, 1)
    for j in range(1, 8):
        got(f"ga{j}")
    send("gas", GA.at[k], GA.at[k], sib)
    w_q0("U", W2)
    w_q1("U", W2)

    def blocks_sum(slot, term):
        def step(b, total):
            return total + term(XT[slot, b].astype(F32)).reshape(FB // 8, 8, TB).sum(0)

        total = lax.fori_loop(0, NB, step, jnp.zeros((8, TB), F32))
        return jnp.sum(total, axis=0, keepdims=True)

    def statistics(slot):
        mean = blocks_sum(slot, lambda v: v) / D
        var = blocks_sum(slot, lambda v: (v - mean) * (v - mean)) / D
        MI[slot, 0:1] = mean
        MI[slot, 1:2] = lax.rsqrt(var + 1e-06)

    tok_done("X", 0)
    statistics(0)
    tok_next("C", CT, 0, 2)
    w_p2("U", W2)
    tok_done("X", 1)
    statistics(1)
    tok_next("C", CT, 1, 2)
    w_r1("U", W2)
    got("gas", "ub")

    def gain_column(kk, zz):
        return GA[kk, zz].T[:FB, 0:1]

    def normalise(b, gw):
        column = gain_column(rem(b, 2), b // 2)
        for slot in range(2):
            v = (XT[slot, b].astype(F32) - MI[slot, 0:1]) * MI[slot, 1:2]
            XN[slot, b] = (v * column).astype(BF)
        return gw

    lax.fori_loop(0, NB // 2, normalise, 0)
    tok_next("C", CT, 0, 3)
    lax.fori_loop(NB // 2, NB, normalise, 0)
    tok_next("C", CT, 1, 3)
    tok_last("C", CT, 0)

    w_done("V")
    GRP = 4

    def panel_dot(W, A, out):
        for j in range(NB // GRP):
            wt = W[j * GRP:(j + 1) * GRP].reshape(GRP * FB, HB).T
            for slot in range(2):
                part = nn_dot(wt, A[slot, j * GRP:(j + 1) * GRP].reshape(GRP * FB, TB))
                if j == 0:
                    out[slot] = part
                else:
                    out[slot] += part

    panel_dot(W1, XN, PRE)
    tok_last("C", CT, 1)
    bias = jnp.where(own, UB[0], UB[2])
    BC[...] = jnp.broadcast_to(bias.T[:, 0:1], (HB, 128))

    CH = 64

    def gelu_rows(i, carry):
        rows = pl.ds(pl.multiple_of(i * CH, CH), CH)
        for slot in range(2):
            v = PRE[slot, rows] + BC[rows, 0:1]
            cdf = 0.5 * (1.0 + lax.erf(v * 0.7071067811865476))
            HID[slot, rows] = (v * cdf).astype(BF)
            SL[slot, rows] = cdf + v * jnp.exp(-0.5 * v * v) * 0.3989422804014327
        return carry

    lax.fori_loop(0, HB // CH, gelu_rows, 0)
    for slot in range(2):
        HIDR[slot] = HID[slot].T

    def z_make(t, W, A, M, S, j):
        pair = rem(z + j + 8, 8)
        w = W[pl.ds(pl.multiple_of(pair * 2, 2), 2)].reshape(2 * FB, HB)
        for slot in range(2):
            part = nn_dot(w, A[slot]).astype(BF)
            M[slot, pair * 2] = part[:FB]
            M[slot, pair * 2 + 1] = part[FB:]
        send(f"{t}s{j}", M.at[:, pair * 2 + 1 - k], S.at[j + 3], sib)

    def z_send(t, M, S, RP, RN, j):
        b = zb(j, k)
        got(f"{t}s{j}")
        for slot in (1, 0):
            total = M[slot, b].astype(F32) + S[j + 3, slot].astype(F32)
            if j == 3 and slot == 0 or j in (1, 2):
                got(f"{t}+{j + 1}{slot}")
                total = total + RP[slot, 3 - j].astype(F32)
            if j == -3 and slot == 1 or j in (-1, -2):
                got(f"{t}-{1 - j}{slot}")
                total = total + RN[slot, 3 + j].astype(F32)
            M[slot, b] = total.astype(BF)
            if j == 4:
                if slot == 0:
                    send(f"{t}+4{slot}", M.at[slot, b], RP.at[slot, 0], zdev(1))
                else:
                    send(f"{t}-4{slot}", M.at[slot, b], RN.at[slot, 0], zdev(-1))
            elif j > 0:
                send(f"{t}+{j}{slot}", M.at[slot, b], RP.at[slot, 4 - j], zdev(1))
            else:
                send(f"{t}-{-j}{slot}", M.at[slot, b], RN.at[slot, 4 + j], zdev(-1))

    def z_total(t, M, S, RP, RN, slot):
        got(f"{t}+1{slot}", f"{t}-1{slot}")
        total = M[slot, b0].astype(F32) + S[3, slot].astype(F32)
        return total + RP[slot, 3].astype(F32) + RN[slot, 3].astype(F32)

    def z_edge(t, M, S, RP, RN, RT):
        got(f"{t}s0")
        M[1, b0] = z_total(t, M, S, RP, RN, 1).astype(BF)
        send(t + "T", M.at[1, b0], RT, tdev)

    def z_final(t, M, S, RP, RN, RT):
        total = z_total(t, M, S, RP, RN, 0)
        got(t + "T")
        return total + RT[...].astype(F32)

    ORDER = (4, 3, -3, 2, -2, 1, -1, 0)
    ma = ("M", MX, MXS, MXP, MXM)
    na = ("N", NG, NGS, NGP, NGM)

    w_done("U")
    for j in ORDER[:3]:
        z_make("M", W2, HID, MX, MXS, j)
    z_send(*ma, 4)
    for j in ORDER[3:]:
        z_make("M", W2, HID, MX, MXS, j)
    tok_done("C", 0)
    tok_done("C", 1)

    yq = 3 - yh

    def g_make(A, B, G, blocks):
        for b in blocks:
            part = nn_dot(A[0, b], B[0]) + nn_dot(A[1, b], B[1])
            G[b] = (part * scale).astype(BF)

    def g_hid(t, G, RY):
        for j in (2, 1, -1, 0):
            b = wb(j, yh)
            send(f"{t}h{j}", G.at[b], RY.at[j + 1], hdev)

    def g_far(t, G, RX, n, yy):
        b = wb(2, yy)
        send(f"{t}{n}2+", G.at[b, lo], RX.at[0, lo], xdev(1))
        send(f"{t}{n}2-", G.at[b, hi], RX.at[0, hi], xdev(-1))

    def g_near(t, G, RX, n, yy):
        for j, tail, rows in ((1, "+", lo), (-1, "-", hi)):
            b = wb(j, yy)
            got(f"{t}{n}2{tail}")
            G[b, rows] = (G[b, rows].astype(F32) + RX[0, rows].astype(F32)).astype(BF)
            send(f"{t}{n}1{tail}", G.at[b], RX.at[1 if j > 0 else 2], xdev(j))

    def g_total(t, G, RX, n, yy):
        got(f"{t}{n}1+", f"{t}{n}1-")
        total = G[wb(0, yy)].astype(F32) + RX[1].astype(F32)
        return total + RX[2].astype(F32)

    def g_add(t, G, RY, j):
        b = wb(j, y)
        got(f"{t}h{j}")
        G[b] = (G[b].astype(F32) + RY[j + 1].astype(F32)).astype(BF)

    def g_step0(t, G, RY, RX):
        g_far(t, G, RX.at[1], "w", yq)
        g_far(t, G, RX.at[2], "t", yt)

    def g_step1(t, G, RY, RX):
        g_add(t, G, RY, 2)
        g_far(t, G, RX.at[0], "o", y)

    def g_step2(t, G, RY, RX):
        g_near(t, G, RX.at[1], "w", yq)
        g_near(t, G, RX.at[2], "t", yt)

    def g_step3(t, G, RY, RX):
        g_add(t, G, RY, 1)
        g_add(t, G, RY, -1)
        g_near(t, G, RX.at[0], "o", y)
        g_add(t, G, RY, 0)

    def g_step4(t, G, RY, RX, T):
        T[0] = g_total(t, G, RX.at[1], "w", yq).astype(BF)
        send(t + "w", T.at[0], RY.at[4], hdev)

    def g_step5(t, G, RY, RX, T, out):
        T[1] = g_total(t, G, RX.at[0], "o", y).astype(BF)
        got(t + "w")
        T[2] = (g_total(t, G, RX.at[2], "t", yt) + RY[4].astype(F32)).astype(BF)
        deliver(t, T.at[1], T.at[2], out)

    def deliver(t, T0, T1, out):
        @pl.when(own)
        def _():
            out[k] = T0[...]
            rc(t + "f1", t + "q1", T1, out.at[k], tdev).start()

        @pl.when(other)
        def _():
            rc(t + "f0", t + "q0", T0, out.at[k], sib).start()
            rc(t + "f1", t + "q2", T1, out.at[k], tdev2).start()

    def finish(t, T0, T1, out):
        @pl.when(own)
        def _():
            rc(t + "f0", t + "q0", T0, out.at[1 - k], sib).wait_recv()

        @pl.when(other)
        def _():
            rc(t + "f1", t + "q1", T1, out.at[k], tdev).wait_recv()
            rc(t + "f1", t + "q2", T1, out.at[1 - k], tdev2).wait_recv()

    def delivered(t, T0, T1, out):
        rc(t + "f1", t + "q1", T1, out.at[k], tdev).wait_send()

        @pl.when(other)
        def _():
            rc(t + "f0", t + "q0", T0, out.at[k], sib).wait_send()

    d2 = ("D", G2, G2Y, G2X)
    d1 = ("E", G1, G1Y, G1X)

    def g_blocks(yy, js=(0, 1, 2, 3)):
        return [wb(j, yy) for j in js]

    g_make(CT, HIDR, G2, g_blocks(yh))
    g_hid("D", G2, G2Y)
    g_make(CT, HIDR, G2, [wb(2, yq), wb(2, yt)])
    g_step0(*d2)
    z_send(*ma, 3)
    z_send(*ma, -3)
    g_make(CT, HIDR, G2, [wb(2, y), wb(1, yq), wb(-1, yq), wb(1, yt), wb(-1, yt)])
    g_step1(*d2)
    panel_dot(W2, CT, HG)
    g_step2(*d2)
    z_send(*ma, 2)
    z_send(*ma, -2)
    g_make(CT, HIDR, G2, [wb(1, y), wb(-1, y), wb(0, yq), wb(0, yt), wb(0, y)])

    def gain_weight(b, total):
        column = gain_column(rem(b, 2), b // 2)
        return total + (W1[b].astype(F32) * column).reshape(FB // 8, 8, HB).sum(0)

    gw = lax.fori_loop(0, NB, gain_weight, jnp.zeros((8, HB), F32))
    gw = jnp.broadcast_to(jnp.sum(gw, axis=0, keepdims=True), (8, HB))
    GW[...] = jnp.broadcast_to(gw.T[:, 0:1], (HB, 128))

    def slope_rows(slot, i, sums):
        first, second = sums
        rows = pl.ds(pl.multiple_of(i * CH, CH), CH)
        grad = (HG[slot, rows] * SL[slot, rows]).astype(BF)
        PG[slot, rows] = grad
        wide = grad.astype(F32)
        first += (wide * GW[rows, 0:1]).reshape(CH // 8, 8, TB).sum(0)
        second += (wide * PRE[slot, rows]).reshape(CH // 8, 8, TB).sum(0)
        return first, second

    zero = jnp.zeros((8, TB), F32)
    line = lax.broadcasted_iota(jnp.int32, (8, TB), 0)
    up_sum = jnp.zeros((1, HB), F32)
    for slot in range(2):
        first, second = lax.fori_loop(0, HB // CH, functools.partial(slope_rows, slot), (zero, zero))
        first = jnp.sum(first, axis=0, keepdims=True)
        second = jnp.sum(second, axis=0, keepdims=True)
        ST[0, slot] = jnp.where(line == 0, first, jnp.where(line == 1, second, 0.0))
        turned = PG[slot].T
        PGR[slot] = turned
        up_sum += jnp.sum(turned.astype(F32), axis=0, keepdims=True)
    send("st", ST.at[0], STS, sib)

    g_make(XN, PGR, G1, g_blocks(yh))
    g_hid("E", G1, G1Y)
    g_make(XN, PGR, G1, [wb(2, yq), wb(2, yt)])
    g_step0(*d1)
    z_make("N", W1, PG, NG, NGS, 4)
    z_send(*ma, 1)
    z_send(*ma, -1)
    g_step3(*d2)
    z_send(*na, 4)
    z_make("N", W1, PG, NG, NGS, 3)
    z_make("N", W1, PG, NG, NGS, -3)
    g_make(XN, PGR, G1, [wb(2, y), wb(1, yq), wb(-1, yq), wb(1, yt), wb(-1, yt)])
    g_step4(*d2, G2T)
    g_step1(*d1)
    for j in ORDER[3:]:
        z_make("N", W1, PG, NG, NGS, j)

    peers8 = [(j, h) for j in range(4) for h in range(2)]

    def bias_row(b):
        v = CT[0, b].astype(F32) + CT[1, b].astype(F32)
        return jnp.sum((v[:, :128] + v[:, 128:]).T, axis=0, keepdims=True)

    for i, (j, h) in enumerate(peers8):
        yy = yh if h else y
        MS[i, :, 0:HB] = jnp.broadcast_to(up_sum, (8, HB))
        MS[i, :, HB:HB + 128] = jnp.zeros((8, 128), F32)
        MS[i, :, HB + 128:] = jnp.zeros((8, 128), F32)
        MS[i, :, HB:HB + FB] = jnp.broadcast_to(bias_row(wb(j, yy)), (8, FB))
        if i:
            send(f"ms{i}", MS.at[i], RM.at[i], dev(rem(x + j, 4), yy, z, k))
    got("st")
    ST[1] = ST[0] + STS[...]
    for j in range(1, 8):
        send(f"st{j}", ST.at[1], STZ.at[j], zdev(j))

    g_make(XN, PGR, G1, [wb(1, y), wb(-1, y), wb(0, yq), wb(0, yt), wb(0, y)])
    z_send(*na, 3)
    z_send(*na, -3)
    g_step2(*d1)
    z_edge(*ma, MXT)
    g_step5(*d2, G2T, G2F)

    total = MS[0]
    for i in range(1, 8):
        got(f"ms{i}")
        total = total + RM[i]
    UT[...] = total[:, :HB]
    dbg_o[...] = total[0:1, HB:HB + FB] * scale
    deliver("B", UT, UT, FU)
    total = ST[1]
    for j in range(1, 8):
        got(f"st{j}")
        total = total + STZ[j]
    ST[2] = total
    send("stt", ST.at[2, 1], STT, tdev)

    z_send(*na, 2)
    z_send(*na, -2)
    mixed = z_final(*ma, MXT).T
    mixed_o[...] = (patches[...].astype(F32) + mixed + dbias[...]).astype(BF)
    g_step3(*d1)
    finish("D", G2T.at[1], G2T.at[2], G2F)
    dw2_o[:HB] = G2F[0].T
    dw2_o[HB:] = G2F[1].T
    finish("B", UT, UT, FU)
    ubg_o[:, :HB] = FU[0, 0:1] * scale
    ubg_o[:, HB:] = FU[1, 0:1] * scale
    z_send(*na, 1)
    z_send(*na, -1)
    g_step4(*d1, G1T)

    got("stt")
    sums = ST[2, 0] + STT[...]
    first = sums[0:1] / D
    second = sums[1:2] / D
    column = gain_column(k, z)
    inv_std = MI[0, 1:2]
    normed = (XT[0, b0].astype(F32) - MI[0, 0:1]) * inv_std

    z_edge(*na, NGT)
    g_step5(*d1, G1T, G1F)
    grad = z_final(*na, NGT)
    product = jnp.sum((grad * normed).T, axis=0, keepdims=True)
    GT[0] = jnp.zeros((8, 256), F32)
    GT[0, :, 0:FB] = jnp.broadcast_to(product, (8, FB))
    for j in range(1, 4):
        send(f"gx{j}", GT.at[0], GTX.at[j], xdev(j))
    correction = grad * column - first - normed * second
    result = CT[0, b0].astype(F32) + inv_std * correction
    pgrad_o[...] = result.T.astype(BF)
    total = GT[0]
    for j in range(1, 4):
        got(f"gx{j}")
        total = total + GTX[j]
    GT[1] = total
    for j in range(1, 4):
        send(f"gy{j}", GT.at[1], GTY.at[j], dev(x, rem(y + j, 4), z, k))
    finish("E", G1T.at[1], G1T.at[2], G1F)
    dw1_o[:, :HB] = G1F[0]
    dw1_o[:, HB:] = G1F[1]
    for j in range(1, 4):
        got(f"gy{j}")
        total = total + GTY[j]
    gaing_o[...] = total[0:1, :FB] * scale

    for copy in made.values():
        copy.wait_send()
    for t, WH, W in (("V", W1H, W1), ("U", W2H, W2)):
        rc(t + "b", t + "u0", WH.at[1 - k], W.at[r], sib).wait_send()

        @pl.when(other)
        def _(t=t, WH=WH, W=W):
            rc(t + "a", t + "u1", WH.at[k], W.at[r], tdev).wait_send()

    delivered("D", G2T.at[1], G2T.at[2], G2F)
    delivered("E", G1T.at[1], G1T.at[2], G1F)
    delivered("B", UT, UT, FU)
    assert len(ids) <= N_SEM


def on_device(patches, norm_gain, up_weight, up_bias, down_weight, down_bias, cotangent):
    scale = 1.0 / math.sqrt(patches.shape[0] * lax.axis_size("row"))
    vm = pltpu.VMEM
    tokens = vm((2, NB, FB, TB), BF)
    panel = vm((NB, FB, HB), BF)
    tile = vm((2, HB, TB), F32)
    ring = vm((2, 4, FB, TB), BF)
    scatter_z = [tokens, vm((8, 2, FB, TB), BF), ring, ring, vm((FB, TB), BF)]
    scatter_w = [panel, vm((5, FB, HB), BF), vm((3, 3, FB, HB), BF), vm((3, FB, HB), BF), vm((2, FB, HB), BF)]
    scratch = [
        tokens, tokens, tokens, panel, panel, vm((2, FB, HB), BF), vm((2, FB, HB), BF),
        vm((2, 8, 8, 256), F32), vm((3, 8, HB), F32), vm((HB, 128), F32), vm((HB, 128), F32), vm((2, 8, TB), F32),
        tile, tile, tile, vm((2, HB, TB), BF), vm((2, HB, TB), BF), vm((2, TB, HB), BF), vm((2, TB, HB), BF),
        *scatter_z, *scatter_z, *scatter_w, *scatter_w,
        vm((3, 2, 8, TB), F32), vm((2, 8, TB), F32), vm((8, 2, 8, TB), F32), vm((8, TB), F32),
        vm((8, 8, HB + 256), F32), vm((8, 8, HB + 256), F32), vm((8, HB), F32), vm((2, 8, HB), F32),
        vm((2, 8, 256), F32), vm((4, 8, 256), F32), vm((4, 8, 256), F32),
        pltpu.SemaphoreType.DMA((N_SEM,)), pltpu.SemaphoreType.DMA((N_SEM,)),
    ]
    shape = jax.ShapeDtypeStruct
    whole = pl.BlockSpec(memory_space=pltpu.VMEM)
    mixed, patch_grad, gain_grad, up_grad, up_bias_grad, down_grad, down_bias_grad = pl.pallas_call(
        functools.partial(kernel, scale),
        out_shape=(
            shape((TB, FB), BF), shape((TB, FB), BF), shape((1, FB), F32), shape((FB, 2 * HB), BF),
            shape((1, 2 * HB), F32), shape((2 * HB, FB), BF), shape((1, FB), F32),
        ),
        in_specs=[whole] * 7,
        out_specs=(whole,) * 7,
        scratch_shapes=scratch,
        compiler_params=pltpu.CompilerParams(
            collective_id=0, has_side_effects=True, vmem_limit_bytes=60 << 20
        ),
        name="mlp_block",
    )(patches, norm_gain[None, :], up_weight, up_bias[None, :], down_weight, down_bias[None, :], cotangent)
    return (
        mixed, patch_grad, gain_grad[0], up_grad, up_bias_grad[0], down_grad, down_bias_grad[0],
    )


def solution(mesh):
    in_specs = (
        P("row", "col"),
        P("col"),
        P("row", "col"),
        P("col"),
        P("col", "row"),
        P("col"),
        P("row", "col"),
    )
    out_specs = (
        P("row", "col"),
        P("row", "col"),
        P("col"),
        P("row", "col"),
        P("col"),
        P("col", "row"),
        P("row"),
    )
    return jax.shard_map(
        on_device, mesh=mesh, in_specs=in_specs, out_specs=out_specs, check_vma=False
    )
```

```python
import functools
import math

import jax
import jax.numpy as jnp
from jax import lax
from jax.experimental import pallas as pl
from jax.experimental.pallas import tpu as pltpu
from jax.sharding import PartitionSpec as P

MESH = pl.DeviceIdType.MESH
BF = jnp.bfloat16
F32 = jnp.float32

NB = 16
FB = 192
TB = 256
HB = 384
D = NB * FB
N_SEM = 320
ORDER = (
    0, 34, 1, 45, 17, 18, 35, 46, 9, 3, 2, 39, 36, 11, 10, 20, 4, 47, 13, 5, 26, 38, 12, 56, 37, 19, 15, 44,
    14, 7, 6, 50, 49, 27, 48, 28, 40, 22, 21, 16, 43, 57, 55, 41, 52, 42, 51, 8, 59, 30, 29, 58, 60, 62, 23,
    54, 24, 53, 63, 32, 31, 61, 64, 66, 25, 33, 149, 65, 116, 115, 86, 83, 67, 150, 88, 87, 119, 151, 68, 85,
    152, 110, 136, 133, 153, 132, 107, 104, 122, 112, 111, 134, 91, 121, 109, 94, 139, 69, 138, 97, 120, 93,
    108, 117, 100, 137, 92, 106, 70, 123, 101, 84, 80, 96, 125, 154, 105, 124, 95, 128, 141, 103, 82, 142,
    140, 99, 155, 156, 72, 73, 102, 145, 127, 98, 118, 113, 81, 77, 126, 76, 130, 143, 71, 79, 75, 135, 147,
    144, 114, 78, 157, 74, 89, 129, 159, 158, 146, 131, 160, 148, 90,
)


def tag(*parts):
    return "".join(map(str, parts))


def rem(a, n):
    return lax.rem(a, n)


def nn_dot(left, right):
    return jnp.dot(left, right, preferred_element_type=F32)


def kernel(
    scale,
    patches, gain, w1in, ubias, w2in, dbias, cot,
    mixed_o, pgrad_o, gaing_o, dw1_o, ubg_o, dw2_o, dbg_o,
    XT, XN, CT, W1, W2, W1H, W2H,
    GIN, UIN, DIN, GA, UB, BC, GW, MI,
    PRE, SL, HG, HID, PG, HIDR, PGR,
    MX, MXS, MXP, MXM, MXT,
    NG, NGS, NGP, NGM, NGT,
    G1, G1Y, G1X, G1T, G1F,
    G2, G2Y, G2X, G2T, G2F,
    ST, STS, STZ, STT,
    MS, RM, UT, FU, GT, GTX, GTY,
    MO, PO, GO, UO, DO,
    ss, rs, ls,
):
    r = lax.axis_index("row")
    c = lax.axis_index("col")
    x, y = r // 4, rem(r, 4)
    z, k = c // 2, rem(c, 2)
    g = y // 2
    yh = y + 1 - 2 * rem(y, 2)
    yt = 3 - y
    yq = 3 - yh
    own = g == k
    other = g != k

    def dev(xx, yy, zz, kk):
        return (xx * 4 + yy, zz * 2 + kk)

    def zdev(j):
        return dev(x, y, rem(z + j + 8, 8), k)

    def xdev(j):
        return dev(rem(x + j + 4, 4), y, z, k)

    sib = dev(x, y, z, 1 - k)
    hdev = dev(x, yh, z, k)
    tdev = dev(x, yt, z, k)
    tdev2 = dev(x, yt, z, 1 - k)
    zp, zm, xp, xm = zdev(1), zdev(-1), xdev(1), xdev(-1)

    def zb(j, kk):
        return rem(z + j + 8, 8) * 2 + kk

    def wb(j, yy):
        return rem(x + j + 4, 4) * 4 + yy

    b0 = zb(0, k)

    barrier = pltpu.get_barrier_semaphore()
    peers = [zdev(j) for j in range(1, 8)] + [xdev(j) for j in range(1, 4)]
    peers += [dev(x, rem(y + j, 4), z, k) for j in range(1, 4)]
    peers += [dev(rem(x + j, 4), yh, z, k) for j in range(1, 4)]
    peers += [sib, tdev2]
    for peer in peers:
        pl.semaphore_signal(barrier, inc=1, device_id=peer, device_id_type=MESH)

    ids = {}
    made = {}
    seen = set()

    def sem(name):
        return ids.setdefault(name, len(ids))

    def rc(sname, rname, src, dst, to):
        return pltpu.make_async_remote_copy(
            src_ref=src, dst_ref=dst, send_sem=ss.at[sem(sname)], recv_sem=rs.at[sem(rname)],
            device_id=to, device_id_type=MESH,
        )

    def send(name, src, dst, to):
        copy = rc(name, name, src, dst, to)
        copy.start()
        made[name] = copy

    def got(*names):
        for name in names:
            if name not in seen:
                seen.add(name)
                made[name].wait_recv()

    local = {}

    def copy_in(name, src, dst):
        local[name] = pltpu.make_async_copy(src, dst, ls.at[len(local)])
        local[name].start()

    copy_in("X", patches, XT.at[0, b0])
    copy_in("V0", w1in.at[:, 0:HB], W1H.at[0])
    copy_in("V1", w1in.at[:, HB:2 * HB], W1H.at[1])
    copy_in("U0", w2in.at[:, 0:HB], W2H.at[0])
    copy_in("U1", w2in.at[:, HB:2 * HB], W2H.at[1])
    copy_in("C", cot, CT.at[0, b0])
    copy_in("g", gain, GIN)
    copy_in("u", ubias, UIN)
    copy_in("d", dbias, DIN)

    tasks = {}

    def task(name, run, *after):
        assert name not in tasks
        tasks[name] = (run, after)

    def gather_tokens(t, A):
        def edge():
            local[t].wait()
            send(t + "T", A.at[0, b0], A.at[1, b0], tdev)

        def first(s):
            if s:
                got(t + "T")
            send(tag(t, "p1", s), A.at[s, b0], A.at[s, b0], zp)
            send(tag(t, "m1", s), A.at[s, b0], A.at[s, b0], zm)
            send(tag(t, "sib0", s), A.at[s, b0], A.at[s, b0], sib)

        def relay(s, n, way):
            b, to, part = (zb(-n, k), zp, lo) if way == "p" else (zb(n, k), zm, hi)
            got(tag(t, way, n, s))
            src = A.at[s, b] if n < 3 else A.at[s, b, part]
            send(tag(t, way, n + 1, s), src, src, to)
            send(tag(t, "sib", way, n, s), A.at[s, b], A.at[s, b], sib)

        def last(s):
            b4 = zb(4, k)
            got(tag(t, "p4", s), tag(t, "m4", s))
            send(tag(t, "sib4", s), A.at[s, b4], A.at[s, b4], sib)

        task(t + "T", edge)
        for s in range(2):
            task(tag(t, "f", s), functools.partial(first, s), t + "T")
            for n in range(1, 4):
                for way in "pm":
                    task(tag(t, way, n, s), functools.partial(relay, s, n, way))
            task(tag(t, "l", s), functools.partial(last, s))

    def tokens_here(t, s):
        for n in ("0", "p1", "m1", "p2", "m2", "p3", "m3", "4"):
            got(tag(t, "sib", n, s))

    lo, hi = pl.ds(0, FB // 2), pl.ds(FB // 2, FB // 2)
    r0, rt, rq = wb(0, y), wb(0, yt), wb(0, yq)

    def gather_panel(t, WH, W):
        def start():
            local[t + "0"].wait()
            local[t + "1"].wait()

            @pl.when(own)
            def _():
                W[r] = WH[k]
                rc(t + "b", t + "u0", WH.at[1 - k], W.at[r], sib).start()

            @pl.when(other)
            def _():
                rc(t + "a", t + "u1", WH.at[k], W.at[r], tdev).start()
                rc(t + "b", t + "u1", WH.at[1 - k], W.at[r], tdev2).start()


        def spread0():
            @pl.when(other)
            def _():
                rc(t + "b", t + "u0", WH.at[1 - k], W.at[r], sib).wait_recv()

            send(t + "P+", W.at[r0], W.at[r0], xp)
            send(t + "P-", W.at[r0], W.at[r0], xm)
            send(t + "Y0", W.at[r0], W.at[r0], hdev)

        def spread1():
            rc(t + "a", t + "u1", WH.at[k], W.at[rt], tdev).wait_recv()
            send(t + "Q0", W.at[rt], W.at[rt], hdev)
            send(t + "Q+", W.at[rt], W.at[rt], xp)
            send(t + "Q-", W.at[rt], W.at[rt], xm)

        def spread2():
            got(t + "Q0")
            send(t + "R+", W.at[rq], W.at[rq], xp)
            send(t + "R-", W.at[rq], W.at[rq], xm)

        def relay(n, yy, way):
            b, to, part, y_name = (wb(-1, yy), xp, lo, "Y1") if way == "+" else (wb(1, yy), xm, hi, "Y2")
            got(tag(t, n, way))
            send(tag(t, n, "2", way), W.at[b, part], W.at[b, part], to)
            if n == "P":
                send(t + y_name, W.at[b], W.at[b], hdev)

        def last():
            b = wb(2, y)
            got(t + "P2+", t + "P2-")
            send(t + "Y3", W.at[b], W.at[b], hdev)

        task(t + "s", start)
        task(t + "0", spread0, t + "s")
        task(t + "1", spread1, t + "s")
        task(t + "2", spread2, t + "s")
        for n, yy in (("P", y), ("Q", yt), ("R", yq)):
            for way in "+-":
                task(t + n + way, functools.partial(relay, n, yy, way))
        task(t + "l", last)

    def panel_here(t):
        got(*(t + n for n in ("Q2+", "Q2-", "R2+", "R2-", "Y0", "Y1", "Y2", "Y3")))

    gather_tokens("X", XT)
    gather_tokens("C", CT)
    gather_panel("V", W1H, W1)
    gather_panel("U", W2H, W2)

    def small_start():
        for name in "gud":
            local[name].wait()
        GA[k, z] = jnp.zeros((1, 256), F32)
        GA[k, z, :, 0:FB] = GIN[...]
        halves = [jnp.concatenate([UIN[i:i + 1] for i in range(n, n + 3)], axis=1) for n in (0, 3)]
        UB[k] = halves[0]
        UB[1 - k] = halves[1]
        send("ub", UB.at[1], UB.at[2], sib)
        for j in range(1, 8):
            send(tag("ga", j), GA.at[k, z], GA.at[k, z], zdev(j))

    def small_next():
        for j in range(1, 8):
            got(tag("ga", j))
        send("gas", GA.at[k], GA.at[k], sib)

    task("ga", small_start)
    task("gb", small_next, "ga")

    def blocks_sum(slot, term):
        def step(b, total):
            return total + term(XT[slot, b].astype(F32)).reshape(FB // 8, 8, TB).sum(0)

        total = lax.fori_loop(0, NB, step, jnp.zeros((8, TB), F32))
        return jnp.sum(total, axis=0, keepdims=True)

    def statistics(slot):
        tokens_here("X", slot)
        mean = blocks_sum(slot, lambda v: v) / D
        var = blocks_sum(slot, lambda v: (v - mean) * (v - mean)) / D
        MI[slot, 0:1] = mean
        MI[slot, 1:2] = lax.rsqrt(var + 1e-06)

    def gain_column(kk, zz):
        return jnp.broadcast_to(GA[kk, zz], (8, 256)).T[:FB, 0:1]

    def normalise(part):
        got("gas", "ub")

        def block(b, carry):
            column = gain_column(rem(b, 2), b // 2)
            for slot in range(2):
                v = (XT[slot, b].astype(F32) - MI[slot, 0:1]) * MI[slot, 1:2]
                XN[slot, b] = (v * column).astype(BF)
            return carry

        lax.fori_loop(part * 4, part * 4 + 4, block, 0)

    task("st0", functools.partial(statistics, 0), "Xl0")
    task("st1", functools.partial(statistics, 1), "Xl1")
    for part in range(4):
        task(tag("nm", part), functools.partial(normalise, part), "st0", "st1", "gb")

    GRP = 4

    def panel_dot(W, A, out):
        for j in range(NB // GRP):
            wt = W[j * GRP:(j + 1) * GRP].reshape(GRP * FB, HB).T
            for slot in range(2):
                part = nn_dot(wt, A[slot, j * GRP:(j + 1) * GRP].reshape(GRP * FB, TB))
                if j == 0:
                    out[slot] = part
                else:
                    out[slot] += part

    def first_product():
        panel_here("V")
        panel_dot(W1, XN, PRE)
        bias = jnp.where(own, UB[0], UB[2])
        BC[...] = jnp.broadcast_to(jnp.broadcast_to(bias, (8, HB)).T[:, 0:1], (HB, 128))

    CH = 64

    def gelu_rows(slot, i, carry):
        rows = pl.ds(pl.multiple_of(i * CH, CH), CH)
        v = PRE[slot, rows] + jnp.concatenate([BC[rows]] * 2, axis=1)
        cdf = 0.5 * (1.0 + lax.erf(v * 0.7071067811865476))
        HID[slot, rows] = (v * cdf).astype(BF)
        SL[slot, rows] = cdf + v * jnp.exp(-0.5 * v * v) * 0.3989422804014327
        return carry

    def gelu(slot):
        lax.fori_loop(0, HB // CH, functools.partial(gelu_rows, slot), 0)
        HIDR[slot] = HID[slot].T

    task("pre", first_product, "nm0", "nm1", "nm2", "nm3", "V0", "V1", "V2", "Vl", "VP+", "VP-", "VQ+", "VQ-", "VR+", "VR-")
    task("ge0", functools.partial(gelu, 0), "pre")
    task("ge1", functools.partial(gelu, 1), "pre")

    def scatter_tokens(t, W, A, M, S, RP, RN, RT, finish, *after):
        def make(j):
            if t == "M":
                panel_here("U")
            pair = rem(z + j + 8, 8)
            w = W[pl.ds(pl.multiple_of(pair * 2, 2), 2)].reshape(2 * FB, HB)
            for slot in range(2):
                part = nn_dot(w, A[slot]).astype(BF)
                M[slot, pair * 2] = part[:FB]
                M[slot, pair * 2 + 1] = part[FB:]
            send(tag(t, "s", j), M.at[:, pair * 2 + 1 - k], S.at[j + 3], sib)

        def relay(j, slot):
            b = zb(j, k)
            got(tag(t, "s", j))
            total = M[slot, b].astype(F32) + S[j + 3, slot].astype(F32)
            if j == 3 and slot == 0 or j in (1, 2):
                got(tag(t, "+", j + 1, slot))
                total = total + RP[slot, 3 - j].astype(F32)
            if j == -3 and slot == 1 or j in (-1, -2):
                got(tag(t, "-", 1 - j, slot))
                total = total + RN[slot, 3 + j].astype(F32)
            M[slot, b] = total.astype(BF)
            if j > 0 and (j < 4 or slot == 0):
                send(tag(t, "+", j, slot), M.at[slot, b], RP.at[slot, 4 - j], zp)
            else:
                n = abs(j)
                send(tag(t, "-", n, slot), M.at[slot, b], RN.at[slot, 4 - n], zm)

        def summed(slot):
            got(tag(t, "s0"), tag(t, "+1", slot), tag(t, "-1", slot))
            total = M[slot, b0].astype(F32) + S[3, slot].astype(F32)
            return total + RP[slot, 3].astype(F32) + RN[slot, 3].astype(F32)

        def edge():
            M[1, b0] = summed(1).astype(BF)
            send(t + "T", M.at[1, b0], RT, tdev)

        def final():
            total = summed(0)
            got(t + "T")
            finish(total + RT[...].astype(F32))

        for j in range(-3, 5):
            task(tag(t, "k", j), functools.partial(make, j), *after)
            for slot in range(2):
                if j:
                    task(tag(t, j, ".", slot), functools.partial(relay, j, slot), tag(t, "k", j))
        task(t + "e", edge, t + "k0")
        task(t + "f", final, t + "k0")

    def finish_mixed(total):
        shift = jnp.broadcast_to(DIN[...], (8, FB)).T[:, 0:1]
        MO[...] = (XT[0, b0].astype(F32) + total + shift).astype(BF)
        copy_in("mo", MO, mixed_o)

    def finish_grad(grad):
        got("stt")
        sums = ST[2, 0] + STT[...]
        inv_std = MI[0, 1:2]
        normed = (XT[0, b0].astype(F32) - MI[0, 0:1]) * inv_std
        product = jnp.sum((grad * normed).T, axis=0, keepdims=True)
        GT[0] = jnp.zeros((1, 256), F32)
        GT[0, :, 0:FB] = product
        for j in range(1, 4):
            send(tag("gx", j), GT.at[0], GTX.at[j], xdev(j))
        correction = grad * gain_column(k, z) - sums[0:1] / D - normed * (sums[1:2] / D)
        PO[...] = (CT[0, b0].astype(F32) + inv_std * correction).astype(BF)
        copy_in("po", PO, pgrad_o)

    UDONE = ("U0", "U1", "U2", "Ul", "UP+", "UP-", "UQ+", "UQ-", "UR+", "UR-")
    scatter_tokens("M", W2, HID, MX, MXS, MXP, MXM, MXT, finish_mixed, "ge0", "ge1", *UDONE)
    scatter_tokens("N", W1, PG, NG, NGS, NGP, NGM, NGT, finish_grad, "sl0", "sl1")

    def deliver(t, T0, T1, out):
        @pl.when(own)
        def _():
            out[k] = T0[...]
            rc(t + "f1", t + "q1", T1, out.at[k], tdev).start()

        @pl.when(other)
        def _():
            rc(t + "f0", t + "q0", T0, out.at[k], sib).start()
            rc(t + "f1", t + "q2", T1, out.at[k], tdev2).start()

    def delivered(t, T0, T1, out):
        @pl.when(own)
        def _():
            rc(t + "f0", t + "q0", T0, out.at[1 - k], sib).wait_recv()

        @pl.when(other)
        def _():
            rc(t + "f1", t + "q1", T1, out.at[k], tdev).wait_recv()
            rc(t + "f1", t + "q2", T1, out.at[1 - k], tdev2).wait_recv()

    def departed(t, T0, T1, out):
        rc(t + "f1", t + "q1", T1, out.at[k], tdev).wait_send()

        @pl.when(other)
        def _():
            rc(t + "f0", t + "q0", T0, out.at[k], sib).wait_send()

    def scatter_panel(t, A, B, G, RY, RX, T, F, out, *after):
        made_here = set()

        def make(*blocks):
            if t == "D":
                tokens_here("C", 0)
                tokens_here("C", 1)
            for j, yy in blocks:
                b = wb(j, yy)
                part = nn_dot(A[0, b], B[0]) + nn_dot(A[1, b], B[1])
                G[b] = (part * scale).astype(BF)

        def hid(j):
            make((j, yh))
            send(tag(t, "h", j), G.at[wb(j, yh)], RY.at[j + 1], hdev)

        def far(n, i, yy):
            make((2, yy))
            b = wb(2, yy)
            if n == "o":
                add(2)
            send(tag(t, n, "2+"), G.at[b, lo], RX.at[i, 0, lo], xp)
            send(tag(t, n, "2-"), G.at[b, hi], RX.at[i, 0, hi], xm)

        def add(j):
            b = wb(j, y)
            got(tag(t, "h", j))
            G[b] = (G[b].astype(F32) + RY[j + 1].astype(F32)).astype(BF)

        def near(n, i, yy, j):
            to, way, part = (xp, "+", lo) if j > 0 else (xm, "-", hi)
            b = wb(j, yy)
            make((j, yy))
            if n == "o":
                add(j)
            got(tag(t, n, "2", way))
            G[b, part] = (G[b, part].astype(F32) + RX[i, 0, part].astype(F32)).astype(BF)
            send(tag(t, n, "1", way), G.at[b], RX.at[i, 1 if j > 0 else 2], to)

        def total(n, i, yy):
            make((0, yy))
            got(tag(t, n, "1+"), tag(t, n, "1-"))
            return G[wb(0, yy)].astype(F32) + RX[i, 1].astype(F32) + RX[i, 2].astype(F32)

        def total_w():
            T[0] = total("w", 1, yq).astype(BF)
            send(t + "w", T.at[0], RY.at[4], hdev)

        def total_o():
            got(tag(t, "h0"))
            T[1] = (total("o", 0, y) + RY[1].astype(F32)).astype(BF)

            @pl.when(own)
            def _():
                F[k] = T[1]

            @pl.when(other)
            def _():
                rc(t + "f0", t + "q0", T.at[1], F.at[k], sib).start()


        def total_t():
            part = total("t", 2, yt)
            got(t + "w")
            T[2] = (part + RY[4].astype(F32)).astype(BF)

            @pl.when(own)
            def _():
                rc(t + "f1", t + "q1", T.at[2], F.at[k], tdev).start()

            @pl.when(other)
            def _():
                rc(t + "f1", t + "q2", T.at[2], F.at[k], tdev2).start()


        def final():
            delivered(t, T.at[1], T.at[2], F)
            copy_in(t + "o0", F.at[0], out.at[:, 0:HB])
            copy_in(t + "o1", F.at[1], out.at[:, HB:2 * HB])

        for j in (2, 1, -1, 0):
            task(tag(t, "h", j), functools.partial(hid, j), *after)
        for n, i, yy in (("w", 1, yq), ("t", 2, yt), ("o", 0, y)):
            task(tag(t, n, "2"), functools.partial(far, n, i, yy), *after)
            for j in (1, -1):
                task(tag(t, n, j), functools.partial(near, n, i, yy, j), *after)
        task(t + "tw", total_w, *after)
        task(t + "to", total_o, *after)
        task(t + "tt", total_t, *after)
        task(t + "f", final, t + "to", t + "tt")

    scatter_panel("D", CT, HIDR, G2, G2Y, G2X, G2T, G2F, dw2_o, "ge0", "ge1", "Cl0", "Cl1")
    scatter_panel("E", XN, PGR, G1, G1Y, G1X, G1T, G1F, dw1_o, "sl0", "sl1")

    def gain_weight():
        def step(b, total):
            column = gain_column(rem(b, 2), b // 2)
            return total + (W1[b].astype(F32) * column).reshape(FB // 8, 8, HB).sum(0)

        got("gas")
        panel_here("V")
        gw = lax.fori_loop(0, NB, step, jnp.zeros((8, HB), F32))
        gw = jnp.broadcast_to(jnp.sum(gw, axis=0, keepdims=True), (8, HB))
        GW[...] = jnp.broadcast_to(gw.T[:, 0:1], (HB, 128))

    def second_product():
        tokens_here("C", 0)
        tokens_here("C", 1)
        panel_here("U")
        panel_dot(W2, CT, HG)

    def slope_rows(slot, i, sums):
        first, second = sums
        rows = pl.ds(pl.multiple_of(i * CH, CH), CH)
        grad = (HG[slot, rows] * SL[slot, rows]).astype(BF)
        PG[slot, rows] = grad
        wide = grad.astype(F32)
        first += (wide * jnp.concatenate([GW[rows]] * 2, axis=1)).reshape(CH // 8, 8, TB).sum(0)
        second += (wide * PRE[slot, rows]).reshape(CH // 8, 8, TB).sum(0)
        return first, second

    up_sums = []

    def slope(slot):
        zero = jnp.zeros((8, TB), F32)
        first, second = lax.fori_loop(0, HB // CH, functools.partial(slope_rows, slot), (zero, zero))
        ST[0, slot, 0:1] = jnp.sum(first, axis=0, keepdims=True)
        ST[0, slot, 1:2] = jnp.sum(second, axis=0, keepdims=True)
        turned = PG[slot].T
        PGR[slot] = turned
        up_sums.append(jnp.sum(turned.astype(F32), axis=0, keepdims=True))

    task("gw", gain_weight, "gb", "pre")
    task("hg", second_product, "Cl0", "Cl1", *UDONE)
    task("sl0", functools.partial(slope, 0), "hg", "ge0", "gw")
    task("sl1", functools.partial(slope, 1), "hg", "ge1", "gw")

    def sums_pair():
        send("st", ST.at[0], STS, sib)

    def sums_z():
        got("st")
        ST[1] = ST[0] + STS[...]
        for j in range(1, 8):
            send(tag("st", j), ST.at[1], STZ.at[j], zdev(j))

    def sums_edge():
        total = ST[1]
        for j in range(1, 8):
            got(tag("st", j))
            total = total + STZ[j]
        ST[2] = total
        send("stt", ST.at[2, 1], STT, tdev)

    task("sa", sums_pair, "sl0", "sl1")
    task("sb", sums_z, "sa")
    task("sc", sums_edge, "sb")

    peers8 = [(j, h) for j in range(4) for h in range(2)]

    def bias_row(b):
        v = CT[0, b].astype(F32) + CT[1, b].astype(F32)
        return jnp.sum((v[:, :128] + v[:, 128:]).T, axis=0, keepdims=True)

    def bias_send():
        for i, (j, h) in enumerate(peers8):
            yy = yh if h else y
            MS[i, :, 0:HB] = up_sums[0] + up_sums[1]
            MS[i, :, HB:HB + 256] = jnp.zeros((1, 256), F32)
            MS[i, :, HB:HB + FB] = bias_row(wb(j, yy))
            if i:
                send(tag("ms", i), MS.at[i], RM.at[i], dev(rem(x + j, 4), yy, z, k))

    def bias_sum():
        total = MS[0]
        for i in range(1, 8):
            got(tag("ms", i))
            total = total + RM[i]
        UT[...] = total[:, :HB]
        DO[...] = total[0:1, HB:HB + FB] * scale
        deliver("B", UT, UT, FU)
        copy_in("do", DO, dbg_o)

    def bias_final():
        delivered("B", UT, UT, FU)
        for i in range(6):
            UO[i:i + 1] = FU[i // 3, 0:1, i % 3 * 128:i % 3 * 128 + 128] * scale
        copy_in("uo", UO, ubg_o)

    task("ba", bias_send, "sl0", "sl1", "hg")
    task("bb", bias_sum, "ba")
    task("bc", bias_final, "bb")

    def gain_y():
        total = GT[0]
        for j in range(1, 4):
            got(tag("gx", j))
            total = total + GTX[j]
        GT[1] = total
        for j in range(1, 4):
            send(tag("gy", j), GT.at[1], GTY.at[j], dev(x, rem(y + j, 4), z, k))

    def gain_final():
        total = GT[1]
        for j in range(1, 4):
            got(tag("gy", j))
            total = total + GTY[j]
        GO[...] = total[0:1, :FB] * scale
        copy_in("go", GO, gaing_o)

    task("gy", gain_y, "Nf")
    task("gz", gain_final, "gy")

    pl.semaphore_wait(barrier, len(peers))
    done = set()
    names = list(tasks)
    for name in (names[i] for i in ORDER):
        run, after = tasks[name]
        assert done.issuperset(after), name
        run()
        done.add(name)
    assert len(done) == len(tasks)

    for name in ("mo", "po", "go", "uo", "do", "Do0", "Do1", "Eo0", "Eo1"):
        local[name].wait()
    for copy in made.values():
        copy.wait_send()
    for t, WH, W in (("V", W1H, W1), ("U", W2H, W2)):
        rc(t + "b", t + "u0", WH.at[1 - k], W.at[r], sib).wait_send()

        @pl.when(other)
        def _(t=t, WH=WH, W=W):
            rc(t + "a", t + "u1", WH.at[k], W.at[r], tdev).wait_send()

    departed("D", G2T.at[1], G2T.at[2], G2F)
    departed("E", G1T.at[1], G1T.at[2], G1F)
    departed("B", UT, UT, FU)
    assert len(ids) <= N_SEM


def hand_over(*refs):
    n = len(refs) // 2
    copies = [pltpu.make_async_copy(refs[i], refs[n + i], refs[-1].at[i]) for i in range(n)]
    for copy in copies:
        copy.start()
    for copy in copies:
        copy.wait()


def on_device(patches, norm_gain, up_weight, up_bias, down_weight, down_bias, cotangent):
    scale = 1.0 / math.sqrt(patches.shape[0] * lax.axis_size("row"))
    vm = pltpu.VMEM
    tokens = vm((2, NB, FB, TB), BF)
    panel = vm((NB, FB, HB), BF)
    tile = vm((2, HB, TB), F32)
    ring = vm((2, 4, FB, TB), BF)
    scatter_z = [tokens, vm((8, 2, FB, TB), BF), ring, ring, vm((FB, TB), BF)]
    scatter_w = [panel, vm((5, FB, HB), BF), vm((3, 3, FB, HB), BF), vm((3, FB, HB), BF), vm((2, FB, HB), BF)]
    scratch = [
        tokens, tokens, tokens, panel, panel, vm((2, FB, HB), BF), vm((2, FB, HB), BF),
        vm((1, FB), F32), vm((6, 128), F32), vm((1, FB), F32),
        vm((2, 8, 1, 256), F32), vm((3, 1, HB), F32), vm((HB, 128), F32), vm((HB, 128), F32), vm((2, 8, TB), F32),
        tile, tile, tile, vm((2, HB, TB), BF), vm((2, HB, TB), BF), vm((2, TB, HB), BF), vm((2, TB, HB), BF),
        *scatter_z, *scatter_z, *scatter_w, *scatter_w,
        vm((3, 2, 2, TB), F32), vm((2, 2, TB), F32), vm((8, 2, 2, TB), F32), vm((2, TB), F32),
        vm((8, 1, HB + 256), F32), vm((8, 1, HB + 256), F32), vm((1, HB), F32), vm((2, 1, HB), F32),
        vm((2, 1, 256), F32), vm((4, 1, 256), F32), vm((4, 1, 256), F32),
        vm((FB, TB), BF), vm((FB, TB), BF), vm((1, FB), F32), vm((6, 128), F32), vm((1, FB), F32),
        pltpu.SemaphoreType.DMA((N_SEM,)), pltpu.SemaphoreType.DMA((N_SEM,)), pltpu.SemaphoreType.DMA((24,)),
    ]
    shape = jax.ShapeDtypeStruct
    whole = pl.BlockSpec(memory_space=pl.ANY)
    results = (
        shape((FB, TB), BF), shape((FB, TB), BF), shape((1, FB), F32), shape((FB, 2 * HB), BF),
        shape((2 * HB // 128, 128), F32), shape((FB, 2 * HB), BF), shape((1, FB), F32),
    )
    parts = pl.pallas_call(
        functools.partial(kernel, scale),
        out_shape=results,
        in_specs=[whole] * 7,
        out_specs=(whole,) * 7,
        scratch_shapes=scratch,
        compiler_params=pltpu.CompilerParams(
            collective_id=0, has_side_effects=True, vmem_limit_bytes=60 << 20
        ),
        name="mlp_block",
    )(
        patches.T, norm_gain[None, :], up_weight, up_bias.reshape(2 * HB // 128, 128),
        down_weight.T, down_bias[None, :], cotangent.T,
    )
    mixed, patch_grad, gain_grad, up_grad, up_bias_grad, down_grad, down_bias_grad = pl.pallas_call(
        hand_over,
        out_shape=results,
        in_specs=[pl.BlockSpec(memory_space=pltpu.VMEM)] * 7,
        out_specs=(whole,) * 7,
        scratch_shapes=[pltpu.SemaphoreType.DMA((7,))],
        name="hand_over",
    )(*parts)
    return (
        mixed.T, patch_grad.T, gain_grad[0], up_grad, up_bias_grad.reshape(2 * HB), down_grad.T, down_bias_grad[0],
    )


def solution(mesh):
    in_specs = (
        P("row", "col"),
        P("col"),
        P("row", "col"),
        P("col"),
        P("col", "row"),
        P("col"),
        P("row", "col"),
    )
    out_specs = (
        P("row", "col"),
        P("row", "col"),
        P("col"),
        P("row", "col"),
        P("col"),
        P("col", "row"),
        P("row"),
    )
    return jax.shard_map(
        on_device, mesh=mesh, in_specs=in_specs, out_specs=out_specs, check_vma=False
    )
```

```python
import functools
import math

import jax
import jax.numpy as jnp
from jax import lax
from jax.experimental import pallas as pl
from jax.experimental.pallas import tpu as pltpu
from jax.sharding import PartitionSpec as P

MESH = pl.DeviceIdType.MESH
BF = jnp.bfloat16
F32 = jnp.float32

NB = 16
FB = 192
TB = 256
HB = 384
D = NB * FB
N_SEM = 320
FEW = 32
REACH = (4, 2)
ORDER = (
    34, 47, 0, 1, 17, 35, 48, 18, 2, 3, 36, 20, 19, 60, 5, 49, 38, 4, 21, 9, 22, 61, 7, 39, 6, 26, 66, 37, 70,
    50, 64, 23, 52, 8, 15, 44, 24, 41, 40, 10, 11, 51, 46, 28, 68, 27, 62, 42, 25, 53, 45, 12, 14, 13, 16, 43,
    54, 31, 32, 63, 65, 58, 56, 67, 69, 29, 55, 71, 57, 30, 33, 72, 74, 59, 73, 123, 126, 130, 127, 157, 78,
    88, 158, 159, 160, 144, 118, 90, 112, 140, 102, 99, 80, 120, 133, 85, 128, 114, 124, 104, 147, 115, 75,
    101, 129, 94, 142, 87, 81, 109, 117, 91, 119, 146, 150, 141, 83, 84, 96, 77, 161, 111, 93, 100, 105, 145,
    131, 116, 132, 107, 162, 97, 95, 136, 149, 125, 148, 103, 108, 113, 164, 153, 76, 92, 121, 163, 134, 143,
    152, 106, 110, 138, 79, 89, 135, 165, 151, 122, 155, 86, 82, 167, 137, 154, 166, 139, 98, 156, 168,
)


def tag(*parts):
    return "".join(map(str, parts))


def rem(a, n):
    return lax.rem(a, n)


def nn_dot(left, right):
    return jnp.dot(left, right, preferred_element_type=F32)


def kernel(
    scale,
    patches, gain, w1in, ubias, w2in, dbias, cot,
    mixed_o, pgrad_o, gaing_o, dw1_o, ubg_o, dw2_o, dbg_o,
    XT, XN, CT, W1, W2, W1H, W2H,
    GIN, UIN, DIN, GA, GF, UB, BC, GW, MI,
    PRE, SL, HG, HID, PG, HIDR, PGR,
    MX, MXS, MXP, MXM, MXT, MXY,
    NG, NGS, NGP, NGM, NGT, NGY,
    G1, G1Y, G1K, G1X, G1T, G1F,
    G2, G2Y, G2K, G2X, G2T, G2F,
    ST, STS, STZ, STT,
    MS, RM, UT, FU, GT, GTX, GTY,
    MO, PO, GO, UO, DO,
    ss, rs, ls,
):
    r = lax.axis_index("row")
    c = lax.axis_index("col")
    x, y = r // 4, rem(r, 4)
    z, k = c // 2, rem(c, 2)
    g = y // 2
    yh = y + 1 - 2 * rem(y, 2)
    yt = 3 - y
    yq = 3 - yh
    own = g == k
    other = g != k

    def dev(xx, yy, zz, kk):
        return (xx * 4 + yy, zz * 2 + kk)

    def zdev(j):
        return dev(x, y, rem(z + j + 8, 8), k)

    def xdev(j):
        return dev(rem(x + j + 4, 4), y, z, k)

    sib = dev(x, y, z, 1 - k)
    hdev = dev(x, yh, z, k)
    tdev = dev(x, yt, z, k)
    tdev2 = dev(x, yt, z, 1 - k)
    zp, zm, xp, xm = zdev(1), zdev(-1), xdev(1), xdev(-1)

    def zb(j, kk):
        return rem(z + j + 8, 8) * 2 + kk

    def wb(j, yy):
        return rem(x + j + 4, 4) * 4 + yy

    b0 = zb(0, k)

    barrier = pltpu.get_barrier_semaphore()
    peers = [zdev(j) for j in range(1, 8)] + [xdev(j) for j in range(1, 4)]
    peers += [dev(x, rem(y + j, 4), z, k) for j in range(1, 4)]
    peers += [dev(rem(x + j, 4), yh, z, k) for j in range(1, 4)]
    peers += [sib, tdev2]
    for peer in peers:
        pl.semaphore_signal(barrier, inc=1, device_id=peer, device_id_type=MESH)

    reach = REACH
    ids = {}
    made = {}
    seen = set()

    def sem(name):
        return ids.setdefault(name, len(ids))

    def rc(sname, rname, src, dst, to):
        return pltpu.make_async_remote_copy(
            src_ref=src, dst_ref=dst, send_sem=ss.at[sem(sname)], recv_sem=rs.at[sem(rname)],
            device_id=to, device_id_type=MESH,
        )

    def send(name, src, dst, to):
        copy = rc(name, name, src, dst, to)
        copy.start()
        made[name] = copy

    def got(*names):
        for name in names:
            if name not in seen:
                seen.add(name)
                made[name].wait_recv()

    local = {}

    def copy_in(name, src, dst):
        local[name] = pltpu.make_async_copy(src, dst, ls.at[len(local)])
        local[name].start()

    copy_in("X", patches, XT.at[0, b0])
    copy_in("V0", w1in.at[:, 0:HB], W1H.at[0])
    copy_in("V1", w1in.at[:, HB:2 * HB], W1H.at[1])
    copy_in("U0", w2in.at[:, 0:HB], W2H.at[0])
    copy_in("U1", w2in.at[:, HB:2 * HB], W2H.at[1])
    copy_in("C", cot, CT.at[0, b0])
    copy_in("g", gain, GIN)
    copy_in("u", ubias, UIN)
    copy_in("d", dbias, DIN)

    tasks = {}

    def task(name, run, *after):
        assert name not in tasks
        tasks[name] = (run, after)

    def gather_tokens(t, A):
        def edge():
            local[t].wait()
            send(t + "T", A.at[0, b0], A.at[1, b0], tdev)

        def first(s):
            if s:
                got(t + "T")
            send(tag(t, "p1", s), A.at[s, b0], A.at[s, b0], zp)
            send(tag(t, "m1", s), A.at[s, b0], A.at[s, b0], zm)
            send(tag(t, "sib0", s), A.at[s, b0], A.at[s, b0], sib)

        def relay(s, n, way):
            b, to, part = (zb(-n, k), zp, lo) if way == "p" else (zb(n, k), zm, hi)
            got(tag(t, way, n, s))
            if n < reach[s]:
                src = A.at[s, b] if n < 3 else A.at[s, b, part]
                send(tag(t, way, n + 1, s), src, src, to)
            if not s and n > reach[1]:
                send(tag(t, "y", way), A.at[0, b], A.at[1, b], tdev)
            send(tag(t, "sib", way, n, s), A.at[s, b], A.at[s, b], sib)

        def across(way):
            b = zb(-3, k) if way == "p" else zb(3, k)
            got(tag(t, "y", way))
            send(tag(t, "sib", way, 3, 1), A.at[1, b], A.at[1, b], sib)

        def last(s):
            b4 = zb(4, k)
            if s and reach[1] < 4:
                got(tag(t, "y"))
            else:
                got(tag(t, "p4", s), tag(t, "m4", s))
            if not s and reach[1] < 4:
                send(tag(t, "y"), A.at[0, b4], A.at[1, b4], tdev)
            send(tag(t, "sib4", s), A.at[s, b4], A.at[s, b4], sib)

        task(t + "T", edge)
        for s in range(2):
            task(tag(t, "f", s), functools.partial(first, s), t + "T")
            for n in range(1, 4):
                for way in "pm":
                    if n <= reach[s]:
                        task(tag(t, way, n, s), functools.partial(relay, s, n, way))
                    else:
                        task(tag(t, way, n, s), functools.partial(across, way))
            task(tag(t, "l", s), functools.partial(last, s))

    def tokens_here(t, s):
        for n in ("0", "p1", "m1", "p2", "m2", "p3", "m3", "4"):
            got(tag(t, "sib", n, s))

    lo, hi = pl.ds(0, FB // 2), pl.ds(FB // 2, FB // 2)
    few, most = (pl.ds(0, FEW), pl.ds(FEW, FEW)), pl.ds(2 * FEW, FB - 2 * FEW)
    r0, rt, rq = wb(0, y), wb(0, yt), wb(0, yq)

    def gather_panel(t, WH, W):
        def start():
            local[t + "0"].wait()
            local[t + "1"].wait()

            @pl.when(own)
            def _():
                W[r] = WH[k]
                rc(t + "b", t + "u0", WH.at[1 - k], W.at[r], sib).start()

            @pl.when(other)
            def _():
                rc(t + "a", t + "u1", WH.at[k], W.at[r], tdev).start()
                rc(t + "b", t + "u1", WH.at[1 - k], W.at[r], tdev2).start()


        def spread0():
            @pl.when(other)
            def _():
                rc(t + "b", t + "u0", WH.at[1 - k], W.at[r], sib).wait_recv()

            send(t + "P+", W.at[r0], W.at[r0], xp)
            send(t + "P-", W.at[r0], W.at[r0], xm)
            send(t + "Y0", W.at[r0], W.at[r0], hdev)

        def spread1():
            rc(t + "a", t + "u1", WH.at[k], W.at[rt], tdev).wait_recv()
            send(t + "Q0", W.at[rt], W.at[rt], hdev)
            send(t + "Q+", W.at[rt], W.at[rt], xp)
            send(t + "Q-", W.at[rt], W.at[rt], xm)

        def spread2():
            got(t + "Q0")
            send(t + "R+", W.at[rq], W.at[rq], xp)
            send(t + "R-", W.at[rq], W.at[rq], xm)

        def relay(n, yy, way):
            b, to, part, y_name = (wb(-1, yy), xp, lo, "Y1") if way == "+" else (wb(1, yy), xm, hi, "Y2")
            got(tag(t, n, way))
            send(tag(t, n, "2", way), W.at[b, part], W.at[b, part], to)
            if n == "P":
                send(t + y_name, W.at[b], W.at[b], hdev)

        def last():
            b = wb(2, y)
            got(t + "P2+", t + "P2-")
            send(t + "Y3", W.at[b, most], W.at[b, most], hdev)

        def aside(j):
            b, name, way, to, part = (wb(1, yh), "Y2", "Z-", xm, few[0]) if j > 0 else (wb(-1, yh), "Y1", "Z+", xp, few[1])
            got(t + name)
            send(t + way, W.at[b, part], W.at[b, part], to)

        task(t + "s", start)
        task(t + "0", spread0, t + "s")
        task(t + "1", spread1, t + "s")
        task(t + "2", spread2, t + "s")
        for n, yy in (("P", y), ("Q", yt), ("R", yq)):
            for way in "+-":
                task(t + n + way, functools.partial(relay, n, yy, way))
        task(t + "l", last)
        task(t + "z1", functools.partial(aside, 1))
        task(t + "z2", functools.partial(aside, -1))

    def panel_here(t):
        got(*(t + n for n in ("Q2+", "Q2-", "R2+", "R2-", "Y0", "Y1", "Y2", "Y3", "Z+", "Z-")))

    gather_tokens("X", XT)
    gather_tokens("C", CT)
    gather_panel("V", W1H, W1)
    gather_panel("U", W2H, W2)

    def small_start():
        for name in "gud":
            local[name].wait()
        GA[k, z] = jnp.zeros((1, 256), F32)
        GA[k, z, :, 0:FB] = GIN[...]
        halves = [jnp.concatenate([UIN[i:i + 1] for i in range(n, n + 3)], axis=1) for n in (0, 3)]
        UB[k] = halves[0]
        UB[1 - k] = halves[1]
        send("ub", UB.at[1], UB.at[2], sib)
        for j in range(1, 8):
            send(tag("ga", j), GA.at[k, z], GA.at[k, z], zdev(j))

    def small_next():
        for j in range(1, 8):
            got(tag("ga", j))
        send("gas", GA.at[k], GA.at[k], sib)

    task("ga", small_start)
    task("gb", small_next, "ga")

    def blocks_sum(slot, term):
        def step(b, total):
            return total + term(XT[slot, b].astype(F32)).reshape(FB // 8, 8, TB).sum(0)

        total = lax.fori_loop(0, NB, step, jnp.zeros((8, TB), F32))
        return jnp.sum(total, axis=0, keepdims=True)

    def statistics(slot):
        tokens_here("X", slot)
        mean = blocks_sum(slot, lambda v: v) / D
        var = blocks_sum(slot, lambda v: (v - mean) * (v - mean)) / D
        MI[slot, 0:1] = mean
        MI[slot, 1:2] = lax.rsqrt(var + 1e-06)

    def gain_column(kk, zz):
        return jnp.broadcast_to(GA[kk, zz], (8, 256)).T[:FB, 0:1]

    def gain_lanes(part):
        got("gas")

        def block(b, carry):
            GF[b] = jnp.broadcast_to(gain_column(rem(b, 2), b // 2), (FB, 128))
            return carry

        lax.fori_loop(part * 4, part * 4 + 4, block, 0)

    def normalise(part):
        got("ub")

        def block(b, carry):
            wide = jnp.concatenate([GF[b]] * 2, axis=1)
            for slot in range(2):
                v = (XT[slot, b].astype(F32) - MI[slot, 0:1]) * MI[slot, 1:2]
                XN[slot, b] = (v * wide).astype(BF)
            return carry

        lax.fori_loop(part * 4, part * 4 + 4, block, 0)

    task("st0", functools.partial(statistics, 0), "Xl0")
    task("st1", functools.partial(statistics, 1), "Xl1")
    for part in range(4):
        task(tag("gf", part), functools.partial(gain_lanes, part), "gb")
        task(tag("nm", part), functools.partial(normalise, part), "st0", "st1", tag("gf", part))

    GRP = 4

    def panel_dot(W, A, out):
        for j in range(NB // GRP):
            wt = W[j * GRP:(j + 1) * GRP].reshape(GRP * FB, HB).T
            for slot in range(2):
                part = nn_dot(wt, A[slot, j * GRP:(j + 1) * GRP].reshape(GRP * FB, TB))
                if j == 0:
                    out[slot] = part
                else:
                    out[slot] += part

    def first_product():
        panel_here("V")
        panel_dot(W1, XN, PRE)
        bias = jnp.where(own, UB[0], UB[2])
        BC[...] = jnp.broadcast_to(jnp.broadcast_to(bias, (8, HB)).T[:, 0:1], (HB, 128))

    CH = 64

    def gelu_rows(slot, i, carry):
        rows = pl.ds(pl.multiple_of(i * CH, CH), CH)
        v = PRE[slot, rows] + jnp.concatenate([BC[rows]] * 2, axis=1)
        cdf = 0.5 * (1.0 + lax.erf(v * 0.7071067811865476))
        HID[slot, rows] = (v * cdf).astype(BF)
        SL[slot, rows] = cdf + v * jnp.exp(-0.5 * v * v) * 0.3989422804014327
        return carry

    def gelu(slot):
        lax.fori_loop(0, HB // CH, functools.partial(gelu_rows, slot), 0)
        HIDR[slot] = HID[slot].T

    task("pre", first_product, "nm0", "nm1", "nm2", "nm3", "V0", "V1", "V2", "Vl", "Vz1", "Vz2", "VP+", "VP-", "VQ+", "VQ-", "VR+", "VR-")
    task("ge0", functools.partial(gelu, 0), "pre")
    task("ge1", functools.partial(gelu, 1), "pre")

    def scatter_tokens(t, W, A, M, S, RP, RN, RT, RY, finish, *after):
        def make(j):
            if t == "M":
                panel_here("U")
            pair = rem(z + j + 8, 8)
            w = W[pl.ds(pl.multiple_of(pair * 2, 2), 2)].reshape(2 * FB, HB)
            for slot in range(2):
                part = nn_dot(w, A[slot]).astype(BF)
                M[slot, pair * 2] = part[:FB]
                M[slot, pair * 2 + 1] = part[FB:]
            send(tag(t, "s", j), M.at[:, pair * 2 + 1 - k], S.at[j + 3], sib)

        def relay(j, slot):
            b = zb(j, k)
            n = abs(j)
            got(tag(t, "s", j))
            total = M[slot, b].astype(F32) + S[j + 3, slot].astype(F32)
            if not slot and n > reach[1]:
                got(tag(t, "y", j))
                total = total + RY[{4: 0, 3: 1, -3: 2}[j]].astype(F32)
            if n + 1 < reach[slot] + (reach[slot] < 4):
                sign, R = ("+", RP) if j > 0 else ("-", RN)
                got(tag(t, sign, n + 1, slot))
                total = total + R[slot, 3 - n].astype(F32)
            M[slot, b] = total.astype(BF)
            if n == 3 and slot == 0:
                sign, R, part = ("+", RP, lo) if j > 0 else ("-", RN, hi)
                got(tag(t, sign, 4, slot))
                M[slot, b, part] = (total[part.start:part.start + part.size] + R[slot, 0, part].astype(F32)).astype(BF)
            if n > reach[slot]:
                send(tag(t, "y", j), M.at[slot, b], RY.at[{4: 0, 3: 1, -3: 2}[j]], tdev)
            elif n == 4:
                send(tag(t, "+4", slot), M.at[slot, b, lo], RP.at[slot, 0, lo], zp)
                send(tag(t, "-4", slot), M.at[slot, b, hi], RN.at[slot, 0, hi], zm)
            elif j > 0:
                send(tag(t, "+", n, slot), M.at[slot, b], RP.at[slot, 4 - n], zp)
            else:
                send(tag(t, "-", n, slot), M.at[slot, b], RN.at[slot, 4 - n], zm)

        def summed(slot):
            got(tag(t, "s0"), tag(t, "+1", slot), tag(t, "-1", slot))
            total = M[slot, b0].astype(F32) + S[3, slot].astype(F32)
            return total + RP[slot, 3].astype(F32) + RN[slot, 3].astype(F32)

        def edge():
            M[1, b0] = summed(1).astype(BF)
            send(t + "T", M.at[1, b0], RT, tdev)

        def final():
            total = summed(0)
            got(t + "T")
            finish(total + RT[...].astype(F32))

        for j in range(-3, 5):
            task(tag(t, "k", j), functools.partial(make, j), *after)
            for slot in range(2):
                if j:
                    task(tag(t, j, ".", slot), functools.partial(relay, j, slot), tag(t, "k", j))
        task(t + "e", edge, t + "k0")
        task(t + "f", final, t + "k0")

    def finish_mixed(total):
        shift = jnp.broadcast_to(DIN[...], (8, FB)).T[:, 0:1]
        MO[...] = (XT[0, b0].astype(F32) + total + shift).astype(BF)
        copy_in("mo", MO, mixed_o)

    def finish_grad(grad):
        got("stt")
        sums = ST[2, 0] + STT[...]
        inv_std = MI[0, 1:2]
        normed = (XT[0, b0].astype(F32) - MI[0, 0:1]) * inv_std
        product = jnp.sum((grad * normed).T, axis=0, keepdims=True)
        GT[0] = jnp.zeros((1, 256), F32)
        GT[0, :, 0:FB] = product
        for j in range(1, 4):
            send(tag("gx", j), GT.at[0], GTX.at[j], xdev(j))
        correction = grad * jnp.concatenate([GF[b0]] * 2, axis=1) - sums[0:1] / D - normed * (sums[1:2] / D)
        PO[...] = (CT[0, b0].astype(F32) + inv_std * correction).astype(BF)
        copy_in("po", PO, pgrad_o)

    UDONE = ("U0", "U1", "U2", "Ul", "Uz1", "Uz2", "UP+", "UP-", "UQ+", "UQ-", "UR+", "UR-")
    scatter_tokens("M", W2, HID, MX, MXS, MXP, MXM, MXT, MXY, finish_mixed, "ge0", "ge1", *UDONE)
    scatter_tokens("N", W1, PG, NG, NGS, NGP, NGM, NGT, NGY, finish_grad, "sl0", "sl1")

    def deliver(t, T0, T1, out):
        @pl.when(own)
        def _():
            out[k] = T0[...]
            rc(t + "f1", t + "q1", T1, out.at[k], tdev).start()

        @pl.when(other)
        def _():
            rc(t + "f0", t + "q0", T0, out.at[k], sib).start()
            rc(t + "f1", t + "q2", T1, out.at[k], tdev2).start()

    def delivered(t, T0, T1, out):
        @pl.when(own)
        def _():
            rc(t + "f0", t + "q0", T0, out.at[1 - k], sib).wait_recv()

        @pl.when(other)
        def _():
            rc(t + "f1", t + "q1", T1, out.at[k], tdev).wait_recv()
            rc(t + "f1", t + "q2", T1, out.at[1 - k], tdev2).wait_recv()

    def departed(t, T0, T1, out):
        rc(t + "f1", t + "q1", T1, out.at[k], tdev).wait_send()

        @pl.when(other)
        def _():
            rc(t + "f0", t + "q0", T0, out.at[k], sib).wait_send()

    def scatter_panel(t, A, B, G, RY, RK, RX, T, F, out, *after):
        made_here = set()

        def make(*blocks):
            if t == "D":
                tokens_here("C", 0)
                tokens_here("C", 1)
            for j, yy in blocks:
                b = wb(j, yy)
                part = nn_dot(A[0, b], B[0]) + nn_dot(A[1, b], B[1])
                G[b] = (part * scale).astype(BF)

        def hid(j):
            make((j, yh))
            b = wb(j, yh)
            if j == 2:
                send(t + "k+", G.at[b, few[0]], RK.at[0], xp)
                send(t + "k-", G.at[b, few[1]], RK.at[1], xm)
                send(tag(t, "h", j), G.at[b, most], RY.at[3, most], hdev)
                return
            if j:
                i, name = (0, "k+") if j > 0 else (1, "k-")
                got(t + name)
                G[b, few[i]] = (G[b, few[i]].astype(F32) + RK[i].astype(F32)).astype(BF)
            send(tag(t, "h", j), G.at[b], RY.at[j + 1], hdev)

        def far(n, i, yy):
            make((2, yy))
            b = wb(2, yy)
            if n == "o":
                add(2)
            send(tag(t, n, "2+"), G.at[b, lo], RX.at[i, 0, lo], xp)
            send(tag(t, n, "2-"), G.at[b, hi], RX.at[i, 0, hi], xm)

        def add(j):
            b = wb(j, y)
            got(tag(t, "h", j))
            rows = most if j == 2 else pl.ds(0, FB)
            G[b, rows] = (G[b, rows].astype(F32) + RY[j + 1, rows].astype(F32)).astype(BF)

        def near(n, i, yy, j):
            to, way, part = (xp, "+", lo) if j > 0 else (xm, "-", hi)
            b = wb(j, yy)
            make((j, yy))
            if n == "o":
                add(j)
            got(tag(t, n, "2", way))
            G[b, part] = (G[b, part].astype(F32) + RX[i, 0, part].astype(F32)).astype(BF)
            send(tag(t, n, "1", way), G.at[b], RX.at[i, 1 if j > 0 else 2], to)

        def total(n, i, yy):
            make((0, yy))
            got(tag(t, n, "1+"), tag(t, n, "1-"))
            return G[wb(0, yy)].astype(F32) + RX[i, 1].astype(F32) + RX[i, 2].astype(F32)

        def total_w():
            T[0] = total("w", 1, yq).astype(BF)
            send(t + "w", T.at[0], RY.at[4], hdev)

        def total_o():
            got(tag(t, "h0"))
            T[1] = (total("o", 0, y) + RY[1].astype(F32)).astype(BF)

            @pl.when(own)
            def _():
                F[k] = T[1]

            @pl.when(other)
            def _():
                rc(t + "f0", t + "q0", T.at[1], F.at[k], sib).start()


        def total_t():
            part = total("t", 2, yt)
            got(t + "w")
            T[2] = (part + RY[4].astype(F32)).astype(BF)

            @pl.when(own)
            def _():
                rc(t + "f1", t + "q1", T.at[2], F.at[k], tdev).start()

            @pl.when(other)
            def _():
                rc(t + "f1", t + "q2", T.at[2], F.at[k], tdev2).start()


        def final():
            delivered(t, T.at[1], T.at[2], F)
            copy_in(t + "o0", F.at[0], out.at[:, 0:HB])
            copy_in(t + "o1", F.at[1], out.at[:, HB:2 * HB])

        for j in (2, 1, -1, 0):
            task(tag(t, "h", j), functools.partial(hid, j), *after)
        for n, i, yy in (("w", 1, yq), ("t", 2, yt), ("o", 0, y)):
            task(tag(t, n, "2"), functools.partial(far, n, i, yy), *after)
            for j in (1, -1):
                task(tag(t, n, j), functools.partial(near, n, i, yy, j), *after)
        task(t + "tw", total_w, *after)
        task(t + "to", total_o, *after)
        task(t + "tt", total_t, *after)
        task(t + "f", final, t + "to", t + "tt")

    scatter_panel("D", CT, HIDR, G2, G2Y, G2K, G2X, G2T, G2F, dw2_o, "ge0", "ge1", "Cl0", "Cl1")
    scatter_panel("E", XN, PGR, G1, G1Y, G1K, G1X, G1T, G1F, dw1_o, "sl0", "sl1")

    def gain_weight():
        def step(b, total):
            wide = jnp.concatenate([GF[b]] * 3, axis=1)
            return total + (W1[b].astype(F32) * wide).reshape(FB // 8, 8, HB).sum(0)

        panel_here("V")
        gw = lax.fori_loop(0, NB, step, jnp.zeros((8, HB), F32))
        gw = jnp.broadcast_to(jnp.sum(gw, axis=0, keepdims=True), (8, HB))
        GW[...] = jnp.broadcast_to(gw.T[:, 0:1], (HB, 128))

    def second_product():
        tokens_here("C", 0)
        tokens_here("C", 1)
        panel_here("U")
        panel_dot(W2, CT, HG)

    def slope_rows(slot, i, sums):
        first, second = sums
        rows = pl.ds(pl.multiple_of(i * CH, CH), CH)
        grad = (HG[slot, rows] * SL[slot, rows]).astype(BF)
        PG[slot, rows] = grad
        wide = grad.astype(F32)
        first += (wide * jnp.concatenate([GW[rows]] * 2, axis=1)).reshape(CH // 8, 8, TB).sum(0)
        second += (wide * PRE[slot, rows]).reshape(CH // 8, 8, TB).sum(0)
        return first, second

    up_sums = []

    def slope(slot):
        zero = jnp.zeros((8, TB), F32)
        first, second = lax.fori_loop(0, HB // CH, functools.partial(slope_rows, slot), (zero, zero))
        ST[0, slot, 0:1] = jnp.sum(first, axis=0, keepdims=True)
        ST[0, slot, 1:2] = jnp.sum(second, axis=0, keepdims=True)
        turned = PG[slot].T
        PGR[slot] = turned
        up_sums.append(jnp.sum(turned.astype(F32), axis=0, keepdims=True))

    task("gw", gain_weight, "pre")
    task("hg", second_product, "Cl0", "Cl1", *UDONE)
    task("sl0", functools.partial(slope, 0), "hg", "ge0", "gw")
    task("sl1", functools.partial(slope, 1), "hg", "ge1", "gw")

    def sums_pair():
        send("st", ST.at[0], STS, sib)

    def sums_z():
        got("st")
        ST[1] = ST[0] + STS[...]
        for j in range(1, 8):
            send(tag("st", j), ST.at[1], STZ.at[j], zdev(j))

    def sums_edge():
        total = ST[1]
        for j in range(1, 8):
            got(tag("st", j))
            total = total + STZ[j]
        ST[2] = total
        send("stt", ST.at[2, 1], STT, tdev)

    task("sa", sums_pair, "sl0", "sl1")
    task("sb", sums_z, "sa")
    task("sc", sums_edge, "sb")

    peers8 = [(j, h) for j in range(4) for h in range(2)]

    def bias_row(b):
        v = CT[0, b].astype(F32) + CT[1, b].astype(F32)
        return jnp.sum((v[:, :128] + v[:, 128:]).T, axis=0, keepdims=True)

    def bias_send():
        for i, (j, h) in enumerate(peers8):
            yy = yh if h else y
            MS[i, :, 0:HB] = up_sums[0] + up_sums[1]
            MS[i, :, HB:HB + 256] = jnp.zeros((1, 256), F32)
            MS[i, :, HB:HB + FB] = bias_row(wb(j, yy))
            if i:
                send(tag("ms", i), MS.at[i], RM.at[i], dev(rem(x + j, 4), yy, z, k))

    def bias_sum():
        total = MS[0]
        for i in range(1, 8):
            got(tag("ms", i))
            total = total + RM[i]
        UT[...] = total[:, :HB]
        DO[...] = total[0:1, HB:HB + FB] * scale
        deliver("B", UT, UT, FU)
        copy_in("do", DO, dbg_o)

    def bias_final():
        delivered("B", UT, UT, FU)
        for i in range(6):
            UO[i:i + 1] = FU[i // 3, 0:1, i % 3 * 128:i % 3 * 128 + 128] * scale
        copy_in("uo", UO, ubg_o)

    task("ba", bias_send, "sl0", "sl1", "hg")
    task("bb", bias_sum, "ba")
    task("bc", bias_final, "bb")

    def gain_y():
        total = GT[0]
        for j in range(1, 4):
            got(tag("gx", j))
            total = total + GTX[j]
        GT[1] = total
        for j in range(1, 4):
            send(tag("gy", j), GT.at[1], GTY.at[j], dev(x, rem(y + j, 4), z, k))

    def gain_final():
        total = GT[1]
        for j in range(1, 4):
            got(tag("gy", j))
            total = total + GTY[j]
        GO[...] = total[0:1, :FB] * scale
        copy_in("go", GO, gaing_o)

    task("gy", gain_y, "Nf")
    task("gz", gain_final, "gy")

    pl.semaphore_wait(barrier, len(peers))
    done = set()
    names = list(tasks)
    for name in (names[i] for i in ORDER):
        run, after = tasks[name]
        assert done.issuperset(after), name
        run()
        done.add(name)
    assert len(done) == len(tasks)

    for name in ("mo", "po", "go", "uo", "do", "Do0", "Do1", "Eo0", "Eo1"):
        local[name].wait()
    for copy in made.values():
        copy.wait_send()
    for t, WH, W in (("V", W1H, W1), ("U", W2H, W2)):
        rc(t + "b", t + "u0", WH.at[1 - k], W.at[r], sib).wait_send()

        @pl.when(other)
        def _(t=t, WH=WH, W=W):
            rc(t + "a", t + "u1", WH.at[k], W.at[r], tdev).wait_send()

    departed("D", G2T.at[1], G2T.at[2], G2F)
    departed("E", G1T.at[1], G1T.at[2], G1F)
    departed("B", UT, UT, FU)
    assert len(ids) <= N_SEM


def hand_over(*refs):
    n = len(refs) // 2
    copies = [pltpu.make_async_copy(refs[i], refs[n + i], refs[-1].at[i]) for i in range(n)]
    for copy in copies:
        copy.start()
    for copy in copies:
        copy.wait()


def on_device(patches, norm_gain, up_weight, up_bias, down_weight, down_bias, cotangent):
    scale = 1.0 / math.sqrt(patches.shape[0] * lax.axis_size("row"))
    vm = pltpu.VMEM
    tokens = vm((2, NB, FB, TB), BF)
    panel = vm((NB, FB, HB), BF)
    tile = vm((2, HB, TB), F32)
    ring = vm((2, 4, FB, TB), BF)
    scatter_z = [tokens, vm((8, 2, FB, TB), BF), ring, ring, vm((FB, TB), BF), vm((3, FB, TB), BF)]
    scatter_w = [panel, vm((5, FB, HB), BF), vm((2, FEW, HB), BF), vm((3, 3, FB, HB), BF), vm((3, FB, HB), BF), vm((2, FB, HB), BF)]
    scratch = [
        tokens, tokens, tokens, panel, panel, vm((2, FB, HB), BF), vm((2, FB, HB), BF),
        vm((1, FB), F32), vm((6, 128), F32), vm((1, FB), F32),
        vm((2, 8, 1, 256), F32), vm((NB, FB, 128), F32), vm((3, 1, HB), F32), vm((HB, 128), F32), vm((HB, 128), F32), vm((2, 8, TB), F32),
        tile, tile, tile, vm((2, HB, TB), BF), vm((2, HB, TB), BF), vm((2, TB, HB), BF), vm((2, TB, HB), BF),
        *scatter_z, *scatter_z, *scatter_w, *scatter_w,
        vm((3, 2, 2, TB), F32), vm((2, 2, TB), F32), vm((8, 2, 2, TB), F32), vm((2, TB), F32),
        vm((8, 1, HB + 256), F32), vm((8, 1, HB + 256), F32), vm((1, HB), F32), vm((2, 1, HB), F32),
        vm((2, 1, 256), F32), vm((4, 1, 256), F32), vm((4, 1, 256), F32),
        vm((FB, TB), BF), vm((FB, TB), BF), vm((1, FB), F32), vm((6, 128), F32), vm((1, FB), F32),
        pltpu.SemaphoreType.DMA((N_SEM,)), pltpu.SemaphoreType.DMA((N_SEM,)), pltpu.SemaphoreType.DMA((24,)),
    ]
    shape = jax.ShapeDtypeStruct
    whole = pl.BlockSpec(memory_space=pl.ANY)
    results = (
        shape((FB, TB), BF), shape((FB, TB), BF), shape((1, FB), F32), shape((FB, 2 * HB), BF),
        shape((2 * HB // 128, 128), F32), shape((FB, 2 * HB), BF), shape((1, FB), F32),
    )
    parts = pl.pallas_call(
        functools.partial(kernel, scale),
        out_shape=results,
        in_specs=[whole] * 7,
        out_specs=(whole,) * 7,
        scratch_shapes=scratch,
        compiler_params=pltpu.CompilerParams(
            collective_id=0, has_side_effects=True, vmem_limit_bytes=60 << 20
        ),
        name="mlp_block",
    )(
        patches.T, norm_gain[None, :], up_weight, up_bias.reshape(2 * HB // 128, 128),
        down_weight.T, down_bias[None, :], cotangent.T,
    )
    mixed, patch_grad, gain_grad, up_grad, up_bias_grad, down_grad, down_bias_grad = pl.pallas_call(
        hand_over,
        out_shape=results,
        in_specs=[pl.BlockSpec(memory_space=pltpu.VMEM)] * 7,
        out_specs=(whole,) * 7,
        scratch_shapes=[pltpu.SemaphoreType.DMA((7,))],
        name="hand_over",
    )(*parts)
    return (
        mixed.T, patch_grad.T, gain_grad[0], up_grad, up_bias_grad.reshape(2 * HB), down_grad.T, down_bias_grad[0],
    )


def solution(mesh):
    in_specs = (
        P("row", "col"),
        P("col"),
        P("row", "col"),
        P("col"),
        P("col", "row"),
        P("col"),
        P("row", "col"),
    )
    out_specs = (
        P("row", "col"),
        P("row", "col"),
        P("col"),
        P("row", "col"),
        P("col"),
        P("col", "row"),
        P("row"),
    )
    return jax.shard_map(
        on_device, mesh=mesh, in_specs=in_specs, out_specs=out_specs, check_vma=False
    )
```

```python
import functools
import math

import jax
import jax.numpy as jnp
from jax import lax
from jax.experimental import pallas as pl
from jax.experimental.pallas import tpu as pltpu
from jax.sharding import PartitionSpec as P

MESH = pl.DeviceIdType.MESH
BF = jnp.bfloat16
F32 = jnp.float32

NB = 16
FB = 192
TB = 256
HB = 384
D = NB * FB
N_SEM = 320
FEW = 32
REACH = (4, 2)
ORDER = (
    34, 47, 0, 1, 17, 35, 48, 18, 2, 3, 36, 20, 19, 60, 5, 49, 38, 4, 21, 9, 22, 61, 7, 39, 6, 26, 66, 37, 70,
    50, 64, 23, 52, 8, 15, 44, 24, 41, 40, 10, 11, 51, 46, 28, 68, 27, 62, 42, 25, 53, 45, 12, 14, 13, 16, 43,
    54, 31, 32, 63, 65, 58, 56, 67, 69, 29, 55, 71, 57, 30, 33, 72, 74, 59, 73, 123, 126, 130, 127, 157, 78,
    88, 158, 159, 160, 144, 118, 90, 112, 140, 102, 99, 80, 120, 133, 85, 128, 114, 124, 104, 147, 115, 75,
    101, 129, 94, 142, 87, 81, 109, 117, 91, 119, 146, 150, 141, 83, 84, 96, 77, 161, 111, 93, 100, 105, 145,
    131, 116, 132, 107, 162, 97, 95, 136, 149, 125, 148, 103, 108, 113, 164, 153, 76, 92, 121, 163, 134, 143,
    152, 106, 110, 138, 79, 89, 135, 165, 151, 122, 155, 86, 82, 167, 137, 154, 166, 139, 98, 156, 168,
)


def tag(*parts):
    return "".join(map(str, parts))


def rem(a, n):
    return lax.rem(a, n)


def nn_dot(left, right):
    return jnp.dot(left, right, preferred_element_type=F32)


def kernel(
    scale,
    patches, gain, w1in, ubias, w2in, dbias, cot,
    mixed_o, pgrad_o, gaing_o, dw1_o, ubg_o, dw2_o, dbg_o,
    XT, XN, CT, W1, W2, W1H, W2H,
    GIN, UIN, DIN, GA, GF, UB, BC, GW, MI,
    PRE, SL, HG, HID, PG, HIDR, PGR,
    MX, MXS, MXP, MXM, MXT, MXY,
    NG, NGS, NGP, NGM, NGT, NGY,
    G1, G1Y, G1K, G1X, G1T, G1F,
    G2, G2Y, G2K, G2X, G2T, G2F,
    ST, STS, STZ, STT,
    MS, RM, UT, FU, GT, GTX, GTY,
    MO, PO, GO, UO, DO,
    ss, rs, ls,
):
    r = lax.axis_index("row")
    c = lax.axis_index("col")
    x, y = r // 4, rem(r, 4)
    z, k = c // 2, rem(c, 2)
    g = y // 2
    yh = y + 1 - 2 * rem(y, 2)
    yt = 3 - y
    yq = 3 - yh
    own = g == k
    other = g != k

    def dev(xx, yy, zz, kk):
        return (xx * 4 + yy, zz * 2 + kk)

    def zdev(j):
        return dev(x, y, rem(z + j + 8, 8), k)

    def xdev(j):
        return dev(rem(x + j + 4, 4), y, z, k)

    sib = dev(x, y, z, 1 - k)
    hdev = dev(x, yh, z, k)
    tdev = dev(x, yt, z, k)
    tdev2 = dev(x, yt, z, 1 - k)
    zp, zm, xp, xm = zdev(1), zdev(-1), xdev(1), xdev(-1)

    def zb(j, kk):
        return rem(z + j + 8, 8) * 2 + kk

    def wb(j, yy):
        return rem(x + j + 4, 4) * 4 + yy

    b0 = zb(0, k)

    barrier = pltpu.get_barrier_semaphore()
    peers = [zdev(j) for j in range(1, 8)] + [xdev(j) for j in range(1, 4)]
    peers += [dev(x, rem(y + j, 4), z, k) for j in range(1, 4)]
    peers += [dev(rem(x + j, 4), yh, z, k) for j in range(1, 4)]
    peers += [sib, tdev2]
    for peer in peers:
        pl.semaphore_signal(barrier, inc=1, device_id=peer, device_id_type=MESH)

    reach = REACH
    ids = {}
    made = {}
    seen = set()

    def sem(name):
        return ids.setdefault(name, len(ids))

    def rc(sname, rname, src, dst, to):
        return pltpu.make_async_remote_copy(
            src_ref=src, dst_ref=dst, send_sem=ss.at[sem(sname)], recv_sem=rs.at[sem(rname)],
            device_id=to, device_id_type=MESH,
        )

    def send(name, src, dst, to):
        copy = rc(name, name, src, dst, to)
        copy.start()
        made[name] = copy

    def got(*names):
        for name in names:
            if name not in seen:
                seen.add(name)
                made[name].wait_recv()

    local = {}

    def copy_in(name, src, dst):
        local[name] = pltpu.make_async_copy(src, dst, ls.at[len(local)])
        local[name].start()

    copy_in("X", patches, XT.at[0, b0])
    copy_in("V0", w1in.at[:, 0:HB], W1H.at[0])
    copy_in("V1", w1in.at[:, HB:2 * HB], W1H.at[1])
    copy_in("U0", w2in.at[:, 0:HB], W2H.at[0])
    copy_in("U1", w2in.at[:, HB:2 * HB], W2H.at[1])
    copy_in("C", cot, CT.at[0, b0])
    copy_in("g", gain, GIN)
    copy_in("u", ubias, UIN)
    copy_in("d", dbias, DIN)

    tasks = {}

    def task(name, run, *after):
        assert name not in tasks
        tasks[name] = (run, after)

    def gather_tokens(t, A):
        def edge():
            local[t].wait()
            send(t + "T", A.at[0, b0], A.at[1, b0], tdev)

        def first(s):
            if s:
                got(t + "T")
            send(tag(t, "p1", s), A.at[s, b0], A.at[s, b0], zp)
            send(tag(t, "m1", s), A.at[s, b0], A.at[s, b0], zm)
            send(tag(t, "sib0", s), A.at[s, b0], A.at[s, b0], sib)

        def relay(s, n, way):
            b, to, part = (zb(-n, k), zp, lo) if way == "p" else (zb(n, k), zm, hi)
            got(tag(t, way, n, s))
            if n < reach[s]:
                src = A.at[s, b] if n < 3 else A.at[s, b, part]
                send(tag(t, way, n + 1, s), src, src, to)
            if not s and n > reach[1]:
                send(tag(t, "y", way), A.at[0, b], A.at[1, b], tdev)
            send(tag(t, "sib", way, n, s), A.at[s, b], A.at[s, b], sib)

        def across(way):
            b = zb(-3, k) if way == "p" else zb(3, k)
            got(tag(t, "y", way))
            send(tag(t, "sib", way, 3, 1), A.at[1, b], A.at[1, b], sib)

        def last(s):
            b4 = zb(4, k)
            if s and reach[1] < 4:
                got(tag(t, "y"))
            else:
                got(tag(t, "p4", s), tag(t, "m4", s))
            if not s and reach[1] < 4:
                send(tag(t, "y"), A.at[0, b4], A.at[1, b4], tdev)
            send(tag(t, "sib4", s), A.at[s, b4], A.at[s, b4], sib)

        task(t + "T", edge)
        for s in range(2):
            task(tag(t, "f", s), functools.partial(first, s), t + "T")
            for n in range(1, 4):
                for way in "pm":
                    if n <= reach[s]:
                        task(tag(t, way, n, s), functools.partial(relay, s, n, way))
                    else:
                        task(tag(t, way, n, s), functools.partial(across, way))
            task(tag(t, "l", s), functools.partial(last, s))

    def tokens_here(t, s):
        for n in ("0", "p1", "m1", "p2", "m2", "p3", "m3", "4"):
            got(tag(t, "sib", n, s))

    lo, hi = pl.ds(0, FB // 2), pl.ds(FB // 2, FB // 2)
    few, most = (pl.ds(0, FEW), pl.ds(FEW, FEW)), pl.ds(2 * FEW, FB - 2 * FEW)
    r0, rt, rq = wb(0, y), wb(0, yt), wb(0, yq)

    def gather_panel(t, WH, W):
        def start():
            local[t + "0"].wait()
            local[t + "1"].wait()

            @pl.when(own)
            def _():
                W[r] = WH[k]
                rc(t + "b", t + "u0", WH.at[1 - k], W.at[r], sib).start()

            @pl.when(other)
            def _():
                rc(t + "a", t + "u1", WH.at[k], W.at[r], tdev).start()
                rc(t + "b", t + "u1", WH.at[1 - k], W.at[r], tdev2).start()


        def spread0():
            @pl.when(other)
            def _():
                rc(t + "b", t + "u0", WH.at[1 - k], W.at[r], sib).wait_recv()

            send(t + "P+", W.at[r0], W.at[r0], xp)
            send(t + "P-", W.at[r0], W.at[r0], xm)
            send(t + "Y0", W.at[r0], W.at[r0], hdev)

        def spread1():
            rc(t + "a", t + "u1", WH.at[k], W.at[rt], tdev).wait_recv()
            send(t + "Q0", W.at[rt], W.at[rt], hdev)
            send(t + "Q+", W.at[rt], W.at[rt], xp)
            send(t + "Q-", W.at[rt], W.at[rt], xm)

        def spread2():
            got(t + "Q0")
            send(t + "R+", W.at[rq], W.at[rq], xp)
            send(t + "R-", W.at[rq], W.at[rq], xm)

        def relay(n, yy, way):
            b, to, part, y_name = (wb(-1, yy), xp, lo, "Y1") if way == "+" else (wb(1, yy), xm, hi, "Y2")
            got(tag(t, n, way))
            send(tag(t, n, "2", way), W.at[b, part], W.at[b, part], to)
            if n == "P":
                send(t + y_name, W.at[b], W.at[b], hdev)

        def last():
            b = wb(2, y)
            got(t + "P2+", t + "P2-")
            send(t + "Y3", W.at[b, most], W.at[b, most], hdev)

        def aside(j):
            b, name, way, to, part = (wb(1, yh), "Y2", "Z-", xm, few[0]) if j > 0 else (wb(-1, yh), "Y1", "Z+", xp, few[1])
            got(t + name)
            send(t + way, W.at[b, part], W.at[b, part], to)

        task(t + "s", start)
        task(t + "0", spread0, t + "s")
        task(t + "1", spread1, t + "s")
        task(t + "2", spread2, t + "s")
        for n, yy in (("P", y), ("Q", yt), ("R", yq)):
            for way in "+-":
                task(t + n + way, functools.partial(relay, n, yy, way))
        task(t + "l", last)
        task(t + "z1", functools.partial(aside, 1))
        task(t + "z2", functools.partial(aside, -1))

    def panel_here(t):
        got(*(t + n for n in ("Q2+", "Q2-", "R2+", "R2-", "Y0", "Y1", "Y2", "Y3", "Z+", "Z-")))

    gather_tokens("X", XT)
    gather_tokens("C", CT)
    gather_panel("V", W1H, W1)
    gather_panel("U", W2H, W2)

    def small_start():
        for name in "gud":
            local[name].wait()
        GA[k, z] = jnp.zeros((1, 256), F32)
        GA[k, z, :, 0:FB] = GIN[...]
        halves = [jnp.concatenate([UIN[i:i + 1] for i in range(n, n + 3)], axis=1) for n in (0, 3)]
        UB[k] = halves[0]
        UB[1 - k] = halves[1]
        send("ub", UB.at[1], UB.at[2], sib)
        for j in range(1, 8):
            send(tag("ga", j), GA.at[k, z], GA.at[k, z], zdev(j))

    def small_next():
        for j in range(1, 8):
            got(tag("ga", j))
        send("gas", GA.at[k], GA.at[k], sib)

    task("ga", small_start)
    task("gb", small_next, "ga")

    def blocks_sum(slot, term):
        def step(b, total):
            return total + term(XT[slot, b].astype(F32)).reshape(FB // 8, 8, TB).sum(0)

        total = lax.fori_loop(0, NB, step, jnp.zeros((8, TB), F32), unroll=4)
        return jnp.sum(total, axis=0, keepdims=True)

    def statistics(slot):
        tokens_here("X", slot)
        mean = blocks_sum(slot, lambda v: v) / D
        var = blocks_sum(slot, lambda v: (v - mean) * (v - mean)) / D
        MI[slot, 0:1] = mean
        MI[slot, 1:2] = lax.rsqrt(var + 1e-06)

    def gain_column(kk, zz):
        return jnp.broadcast_to(GA[kk, zz], (8, 256)).T[:FB, 0:1]

    def gain_lanes(part):
        got("gas")

        def block(b, carry):
            GF[b] = jnp.broadcast_to(gain_column(rem(b, 2), b // 2), (FB, 128))
            return carry

        lax.fori_loop(part * 4, part * 4 + 4, block, 0)

    def normalise(part):
        got("ub")

        def block(b, carry):
            wide = jnp.concatenate([GF[b]] * 2, axis=1)
            for slot in range(2):
                v = (XT[slot, b].astype(F32) - MI[slot, 0:1]) * MI[slot, 1:2]
                XN[slot, b] = (v * wide).astype(BF)
            return carry

        lax.fori_loop(part * 4, part * 4 + 4, block, 0, unroll=2)

    task("st0", functools.partial(statistics, 0), "Xl0")
    task("st1", functools.partial(statistics, 1), "Xl1")
    for part in range(4):
        task(tag("gf", part), functools.partial(gain_lanes, part), "gb")
        task(tag("nm", part), functools.partial(normalise, part), "st0", "st1", tag("gf", part))

    GRP = 4

    def panel_dot(W, A, out):
        for j in range(NB // GRP):
            wt = W[j * GRP:(j + 1) * GRP].reshape(GRP * FB, HB).T
            for slot in range(2):
                part = nn_dot(wt, A[slot, j * GRP:(j + 1) * GRP].reshape(GRP * FB, TB))
                if j == 0:
                    out[slot] = part
                else:
                    out[slot] += part

    def first_product():
        panel_here("V")
        panel_dot(W1, XN, PRE)
        bias = jnp.where(own, UB[0], UB[2])
        BC[...] = jnp.broadcast_to(jnp.broadcast_to(bias, (8, HB)).T[:, 0:1], (HB, 128))

    CH = 64

    def gelu_rows(slot, i, carry):
        rows = pl.ds(pl.multiple_of(i * CH, CH), CH)
        v = PRE[slot, rows] + jnp.concatenate([BC[rows]] * 2, axis=1)
        cdf = 0.5 * (1.0 + lax.erf(v * 0.7071067811865476))
        HID[slot, rows] = (v * cdf).astype(BF)
        SL[slot, rows] = cdf + v * jnp.exp(-0.5 * v * v) * 0.3989422804014327
        return carry

    def gelu(slot):
        lax.fori_loop(0, HB // CH, functools.partial(gelu_rows, slot), 0)
        HIDR[slot] = HID[slot].T

    task("pre", first_product, "nm0", "nm1", "nm2", "nm3", "V0", "V1", "V2", "Vl", "Vz1", "Vz2", "VP+", "VP-", "VQ+", "VQ-", "VR+", "VR-")
    task("ge0", functools.partial(gelu, 0), "pre")
    task("ge1", functools.partial(gelu, 1), "pre")

    def scatter_tokens(t, W, A, M, S, RP, RN, RT, RY, finish, *after):
        def make(j):
            if t == "M":
                panel_here("U")
            pair = rem(z + j + 8, 8)
            w = W[pl.ds(pl.multiple_of(pair * 2, 2), 2)].reshape(2 * FB, HB)
            for slot in range(2):
                part = nn_dot(w, A[slot]).astype(BF)
                M[slot, pair * 2] = part[:FB]
                M[slot, pair * 2 + 1] = part[FB:]
            send(tag(t, "s", j), M.at[:, pair * 2 + 1 - k], S.at[j + 3], sib)

        def relay(j, slot):
            b = zb(j, k)
            n = abs(j)
            got(tag(t, "s", j))
            total = M[slot, b].astype(F32) + S[j + 3, slot].astype(F32)
            if not slot and n > reach[1]:
                got(tag(t, "y", j))
                total = total + RY[{4: 0, 3: 1, -3: 2}[j]].astype(F32)
            if n + 1 < reach[slot] + (reach[slot] < 4):
                sign, R = ("+", RP) if j > 0 else ("-", RN)
                got(tag(t, sign, n + 1, slot))
                total = total + R[slot, 3 - n].astype(F32)
            M[slot, b] = total.astype(BF)
            if n == 3 and slot == 0:
                sign, R, part = ("+", RP, lo) if j > 0 else ("-", RN, hi)
                got(tag(t, sign, 4, slot))
                M[slot, b, part] = (total[part.start:part.start + part.size] + R[slot, 0, part].astype(F32)).astype(BF)
            if n > reach[slot]:
                send(tag(t, "y", j), M.at[slot, b], RY.at[{4: 0, 3: 1, -3: 2}[j]], tdev)
            elif n == 4:
                send(tag(t, "+4", slot), M.at[slot, b, lo], RP.at[slot, 0, lo], zp)
                send(tag(t, "-4", slot), M.at[slot, b, hi], RN.at[slot, 0, hi], zm)
            elif j > 0:
                send(tag(t, "+", n, slot), M.at[slot, b], RP.at[slot, 4 - n], zp)
            else:
                send(tag(t, "-", n, slot), M.at[slot, b], RN.at[slot, 4 - n], zm)

        def summed(slot):
            got(tag(t, "s0"), tag(t, "+1", slot), tag(t, "-1", slot))
            total = M[slot, b0].astype(F32) + S[3, slot].astype(F32)
            return total + RP[slot, 3].astype(F32) + RN[slot, 3].astype(F32)

        def edge():
            M[1, b0] = summed(1).astype(BF)
            send(t + "T", M.at[1, b0], RT, tdev)

        def final():
            total = summed(0)
            got(t + "T")
            finish(total + RT[...].astype(F32))

        for j in range(-3, 5):
            task(tag(t, "k", j), functools.partial(make, j), *after)
            for slot in range(2):
                if j:
                    task(tag(t, j, ".", slot), functools.partial(relay, j, slot), tag(t, "k", j))
        task(t + "e", edge, t + "k0")
        task(t + "f", final, t + "k0")

    def finish_mixed(total):
        shift = jnp.broadcast_to(DIN[...], (8, FB)).T[:, 0:1]
        MO[...] = (XT[0, b0].astype(F32) + total + shift).astype(BF)
        copy_in("mo", MO, mixed_o)

    def finish_grad(grad):
        got("stt")
        sums = ST[2, 0] + STT[...]
        inv_std = MI[0, 1:2]
        normed = (XT[0, b0].astype(F32) - MI[0, 0:1]) * inv_std
        product = jnp.sum((grad * normed).T, axis=0, keepdims=True)
        GT[0] = jnp.zeros((1, 256), F32)
        GT[0, :, 0:FB] = product
        for j in range(1, 4):
            send(tag("gx", j), GT.at[0], GTX.at[j], xdev(j))
        correction = grad * jnp.concatenate([GF[b0]] * 2, axis=1) - sums[0:1] / D - normed * (sums[1:2] / D)
        PO[...] = (CT[0, b0].astype(F32) + inv_std * correction).astype(BF)
        copy_in("po", PO, pgrad_o)

    UDONE = ("U0", "U1", "U2", "Ul", "Uz1", "Uz2", "UP+", "UP-", "UQ+", "UQ-", "UR+", "UR-")
    scatter_tokens("M", W2, HID, MX, MXS, MXP, MXM, MXT, MXY, finish_mixed, "ge0", "ge1", *UDONE)
    scatter_tokens("N", W1, PG, NG, NGS, NGP, NGM, NGT, NGY, finish_grad, "sl0", "sl1")

    def deliver(t, T0, T1, out):
        @pl.when(own)
        def _():
            out[k] = T0[...]
            rc(t + "f1", t + "q1", T1, out.at[k], tdev).start()

        @pl.when(other)
        def _():
            rc(t + "f0", t + "q0", T0, out.at[k], sib).start()
            rc(t + "f1", t + "q2", T1, out.at[k], tdev2).start()

    def delivered(t, T0, T1, out):
        @pl.when(own)
        def _():
            rc(t + "f0", t + "q0", T0, out.at[1 - k], sib).wait_recv()

        @pl.when(other)
        def _():
            rc(t + "f1", t + "q1", T1, out.at[k], tdev).wait_recv()
            rc(t + "f1", t + "q2", T1, out.at[1 - k], tdev2).wait_recv()

    def departed(t, T0, T1, out):
        rc(t + "f1", t + "q1", T1, out.at[k], tdev).wait_send()

        @pl.when(other)
        def _():
            rc(t + "f0", t + "q0", T0, out.at[k], sib).wait_send()

    def scatter_panel(t, A, B, G, RY, RK, RX, T, F, out, *after):
        made_here = set()

        def make(*blocks):
            if t == "D":
                tokens_here("C", 0)
                tokens_here("C", 1)
            for j, yy in blocks:
                b = wb(j, yy)
                part = nn_dot(A[0, b], B[0]) + nn_dot(A[1, b], B[1])
                G[b] = (part * scale).astype(BF)

        def hid(j):
            make((j, yh))
            b = wb(j, yh)
            if j == 2:
                send(t + "k+", G.at[b, few[0]], RK.at[0], xp)
                send(t + "k-", G.at[b, few[1]], RK.at[1], xm)
                send(tag(t, "h", j), G.at[b, most], RY.at[3, most], hdev)
                return
            if j:
                i, name = (0, "k+") if j > 0 else (1, "k-")
                got(t + name)
                G[b, few[i]] = (G[b, few[i]].astype(F32) + RK[i].astype(F32)).astype(BF)
            send(tag(t, "h", j), G.at[b], RY.at[j + 1], hdev)

        def far(n, i, yy):
            make((2, yy))
            b = wb(2, yy)
            if n == "o":
                add(2)
            send(tag(t, n, "2+"), G.at[b, lo], RX.at[i, 0, lo], xp)
            send(tag(t, n, "2-"), G.at[b, hi], RX.at[i, 0, hi], xm)

        def add(j):
            b = wb(j, y)
            got(tag(t, "h", j))
            rows = most if j == 2 else pl.ds(0, FB)
            G[b, rows] = (G[b, rows].astype(F32) + RY[j + 1, rows].astype(F32)).astype(BF)

        def near(n, i, yy, j):
            to, way, part = (xp, "+", lo) if j > 0 else (xm, "-", hi)
            b = wb(j, yy)
            make((j, yy))
            if n == "o":
                add(j)
            got(tag(t, n, "2", way))
            G[b, part] = (G[b, part].astype(F32) + RX[i, 0, part].astype(F32)).astype(BF)
            send(tag(t, n, "1", way), G.at[b], RX.at[i, 1 if j > 0 else 2], to)

        def total(n, i, yy):
            make((0, yy))
            got(tag(t, n, "1+"), tag(t, n, "1-"))
            return G[wb(0, yy)].astype(F32) + RX[i, 1].astype(F32) + RX[i, 2].astype(F32)

        def total_w():
            T[0] = total("w", 1, yq).astype(BF)
            send(t + "w", T.at[0], RY.at[4], hdev)

        def total_o():
            got(tag(t, "h0"))
            T[1] = (total("o", 0, y) + RY[1].astype(F32)).astype(BF)

            @pl.when(own)
            def _():
                F[k] = T[1]

            @pl.when(other)
            def _():
                rc(t + "f0", t + "q0", T.at[1], F.at[k], sib).start()


        def total_t():
            part = total("t", 2, yt)
            got(t + "w")
            T[2] = (part + RY[4].astype(F32)).astype(BF)

            @pl.when(own)
            def _():
                rc(t + "f1", t + "q1", T.at[2], F.at[k], tdev).start()

            @pl.when(other)
            def _():
                rc(t + "f1", t + "q2", T.at[2], F.at[k], tdev2).start()


        def final():
            delivered(t, T.at[1], T.at[2], F)
            copy_in(t + "o0", F.at[0], out.at[:, 0:HB])
            copy_in(t + "o1", F.at[1], out.at[:, HB:2 * HB])

        for j in (2, 1, -1, 0):
            task(tag(t, "h", j), functools.partial(hid, j), *after)
        for n, i, yy in (("w", 1, yq), ("t", 2, yt), ("o", 0, y)):
            task(tag(t, n, "2"), functools.partial(far, n, i, yy), *after)
            for j in (1, -1):
                task(tag(t, n, j), functools.partial(near, n, i, yy, j), *after)
        task(t + "tw", total_w, *after)
        task(t + "to", total_o, *after)
        task(t + "tt", total_t, *after)
        task(t + "f", final, t + "to", t + "tt")

    scatter_panel("D", CT, HIDR, G2, G2Y, G2K, G2X, G2T, G2F, dw2_o, "ge0", "ge1", "Cl0", "Cl1")
    scatter_panel("E", XN, PGR, G1, G1Y, G1K, G1X, G1T, G1F, dw1_o, "sl0", "sl1")

    def gain_weight():
        def step(b, total):
            wide = jnp.concatenate([GF[b]] * 3, axis=1)
            return total + (W1[b].astype(F32) * wide).reshape(FB // 8, 8, HB).sum(0)

        panel_here("V")
        gw = lax.fori_loop(0, NB, step, jnp.zeros((8, HB), F32), unroll=4)
        gw = jnp.broadcast_to(jnp.sum(gw, axis=0, keepdims=True), (8, HB))
        GW[...] = jnp.broadcast_to(gw.T[:, 0:1], (HB, 128))

    def second_product():
        tokens_here("C", 0)
        tokens_here("C", 1)
        panel_here("U")
        panel_dot(W2, CT, HG)

    def slope_rows(slot, i, sums):
        first, second = sums
        rows = pl.ds(pl.multiple_of(i * CH, CH), CH)
        grad = (HG[slot, rows] * SL[slot, rows]).astype(BF)
        PG[slot, rows] = grad
        wide = grad.astype(F32)
        first += (wide * jnp.concatenate([GW[rows]] * 2, axis=1)).reshape(CH // 8, 8, TB).sum(0)
        second += (wide * PRE[slot, rows]).reshape(CH // 8, 8, TB).sum(0)
        return first, second

    up_sums = []

    def slope(slot):
        zero = jnp.zeros((8, TB), F32)
        first, second = lax.fori_loop(0, HB // CH, functools.partial(slope_rows, slot), (zero, zero), unroll=3)
        ST[0, slot, 0:1] = jnp.sum(first, axis=0, keepdims=True)
        ST[0, slot, 1:2] = jnp.sum(second, axis=0, keepdims=True)
        turned = PG[slot].T
        PGR[slot] = turned
        up_sums.append(jnp.sum(turned.astype(F32), axis=0, keepdims=True))

    task("gw", gain_weight, "pre")
    task("hg", second_product, "Cl0", "Cl1", *UDONE)
    task("sl0", functools.partial(slope, 0), "hg", "ge0", "gw")
    task("sl1", functools.partial(slope, 1), "hg", "ge1", "gw")

    def sums_pair():
        send("st", ST.at[0], STS, sib)

    def sums_z():
        got("st")
        ST[1] = ST[0] + STS[...]
        for j in range(1, 8):
            send(tag("st", j), ST.at[1], STZ.at[j], zdev(j))

    def sums_edge():
        total = ST[1]
        for j in range(1, 8):
            got(tag("st", j))
            total = total + STZ[j]
        ST[2] = total
        send("stt", ST.at[2, 1], STT, tdev)

    task("sa", sums_pair, "sl0", "sl1")
    task("sb", sums_z, "sa")
    task("sc", sums_edge, "sb")

    peers8 = [(j, h) for j in range(4) for h in range(2)]

    def bias_row(b):
        v = CT[0, b].astype(F32) + CT[1, b].astype(F32)
        return jnp.sum((v[:, :128] + v[:, 128:]).T, axis=0, keepdims=True)

    def bias_send():
        for i, (j, h) in enumerate(peers8):
            yy = yh if h else y
            MS[i, :, 0:HB] = up_sums[0] + up_sums[1]
            MS[i, :, HB:HB + 256] = jnp.zeros((1, 256), F32)
            MS[i, :, HB:HB + FB] = bias_row(wb(j, yy))
            if i:
                send(tag("ms", i), MS.at[i], RM.at[i], dev(rem(x + j, 4), yy, z, k))

    def bias_sum():
        total = MS[0]
        for i in range(1, 8):
            got(tag("ms", i))
            total = total + RM[i]
        UT[...] = total[:, :HB]
        DO[...] = total[0:1, HB:HB + FB] * scale
        deliver("B", UT, UT, FU)
        copy_in("do", DO, dbg_o)

    def bias_final():
        delivered("B", UT, UT, FU)
        for i in range(6):
            UO[i:i + 1] = FU[i // 3, 0:1, i % 3 * 128:i % 3 * 128 + 128] * scale
        copy_in("uo", UO, ubg_o)

    task("ba", bias_send, "sl0", "sl1", "hg")
    task("bb", bias_sum, "ba")
    task("bc", bias_final, "bb")

    def gain_y():
        total = GT[0]
        for j in range(1, 4):
            got(tag("gx", j))
            total = total + GTX[j]
        GT[1] = total
        for j in range(1, 4):
            send(tag("gy", j), GT.at[1], GTY.at[j], dev(x, rem(y + j, 4), z, k))

    def gain_final():
        total = GT[1]
        for j in range(1, 4):
            got(tag("gy", j))
            total = total + GTY[j]
        GO[...] = total[0:1, :FB] * scale
        copy_in("go", GO, gaing_o)

    task("gy", gain_y, "Nf")
    task("gz", gain_final, "gy")

    pl.semaphore_wait(barrier, len(peers))
    done = set()
    names = list(tasks)
    for name in (names[i] for i in ORDER):
        run, after = tasks[name]
        assert done.issuperset(after), name
        run()
        done.add(name)
    assert len(done) == len(tasks)

    for name in ("mo", "po", "go", "uo", "do", "Do0", "Do1", "Eo0", "Eo1"):
        local[name].wait()
    for copy in made.values():
        copy.wait_send()
    for t, WH, W in (("V", W1H, W1), ("U", W2H, W2)):
        rc(t + "b", t + "u0", WH.at[1 - k], W.at[r], sib).wait_send()

        @pl.when(other)
        def _(t=t, WH=WH, W=W):
            rc(t + "a", t + "u1", WH.at[k], W.at[r], tdev).wait_send()

    departed("D", G2T.at[1], G2T.at[2], G2F)
    departed("E", G1T.at[1], G1T.at[2], G1F)
    departed("B", UT, UT, FU)
    assert len(ids) <= N_SEM


def hand_over(*refs):
    n = len(refs) // 2
    copies = [pltpu.make_async_copy(refs[i], refs[n + i], refs[-1].at[i]) for i in range(n)]
    for copy in copies:
        copy.start()
    for copy in copies:
        copy.wait()


def on_device(patches, norm_gain, up_weight, up_bias, down_weight, down_bias, cotangent):
    scale = 1.0 / math.sqrt(patches.shape[0] * lax.axis_size("row"))
    vm = pltpu.VMEM
    tokens = vm((2, NB, FB, TB), BF)
    panel = vm((NB, FB, HB), BF)
    tile = vm((2, HB, TB), F32)
    ring = vm((2, 4, FB, TB), BF)
    scatter_z = [tokens, vm((8, 2, FB, TB), BF), ring, ring, vm((FB, TB), BF), vm((3, FB, TB), BF)]
    scatter_w = [panel, vm((5, FB, HB), BF), vm((2, FEW, HB), BF), vm((3, 3, FB, HB), BF), vm((3, FB, HB), BF), vm((2, FB, HB), BF)]
    scratch = [
        tokens, tokens, tokens, panel, panel, vm((2, FB, HB), BF), vm((2, FB, HB), BF),
        vm((1, FB), F32), vm((6, 128), F32), vm((1, FB), F32),
        vm((2, 8, 1, 256), F32), vm((NB, FB, 128), F32), vm((3, 1, HB), F32), vm((HB, 128), F32), vm((HB, 128), F32), vm((2, 8, TB), F32),
        tile, tile, tile, vm((2, HB, TB), BF), vm((2, HB, TB), BF), vm((2, TB, HB), BF), vm((2, TB, HB), BF),
        *scatter_z, *scatter_z, *scatter_w, *scatter_w,
        vm((3, 2, 2, TB), F32), vm((2, 2, TB), F32), vm((8, 2, 2, TB), F32), vm((2, TB), F32),
        vm((8, 1, HB + 256), F32), vm((8, 1, HB + 256), F32), vm((1, HB), F32), vm((2, 1, HB), F32),
        vm((2, 1, 256), F32), vm((4, 1, 256), F32), vm((4, 1, 256), F32),
        vm((FB, TB), BF), vm((FB, TB), BF), vm((1, FB), F32), vm((6, 128), F32), vm((1, FB), F32),
        pltpu.SemaphoreType.DMA((N_SEM,)), pltpu.SemaphoreType.DMA((N_SEM,)), pltpu.SemaphoreType.DMA((24,)),
    ]
    shape = jax.ShapeDtypeStruct
    whole = pl.BlockSpec(memory_space=pl.ANY)
    results = (
        shape((FB, TB), BF), shape((FB, TB), BF), shape((1, FB), F32), shape((FB, 2 * HB), BF),
        shape((2 * HB // 128, 128), F32), shape((FB, 2 * HB), BF), shape((1, FB), F32),
    )
    parts = pl.pallas_call(
        functools.partial(kernel, scale),
        out_shape=results,
        in_specs=[whole] * 7,
        out_specs=(whole,) * 7,
        scratch_shapes=scratch,
        compiler_params=pltpu.CompilerParams(
            collective_id=0, has_side_effects=True, vmem_limit_bytes=60 << 20
        ),
        name="mlp_block",
    )(
        patches.T, norm_gain[None, :], up_weight, up_bias.reshape(2 * HB // 128, 128),
        down_weight.T, down_bias[None, :], cotangent.T,
    )
    mixed, patch_grad, gain_grad, up_grad, up_bias_grad, down_grad, down_bias_grad = pl.pallas_call(
        hand_over,
        out_shape=results,
        in_specs=[pl.BlockSpec(memory_space=pltpu.VMEM)] * 7,
        out_specs=(whole,) * 7,
        scratch_shapes=[pltpu.SemaphoreType.DMA((7,))],
        name="hand_over",
    )(*parts)
    return (
        mixed.T, patch_grad.T, gain_grad[0], up_grad, up_bias_grad.reshape(2 * HB), down_grad.T, down_bias_grad[0],
    )


def solution(mesh):
    in_specs = (
        P("row", "col"),
        P("col"),
        P("row", "col"),
        P("col"),
        P("col", "row"),
        P("col"),
        P("row", "col"),
    )
    out_specs = (
        P("row", "col"),
        P("row", "col"),
        P("col"),
        P("row", "col"),
        P("col"),
        P("col", "row"),
        P("row"),
    )
    return jax.shard_map(
        on_device, mesh=mesh, in_specs=in_specs, out_specs=out_specs, check_vma=False
    )
```
